32 devices in a mesh: pipe: 8 (over y, x, core), dp: 4 (over z).
Axes of the slice: x: 2, y: 2, z: 4, core: 2. Of those that a mesh axis runs over, the one named last changes fastest.
Arguments:
- section_inputs: bfloat16 [8, 2, 256, 4096], P('pipe', None, 'dp'), may hold values from -6 to 6
- arriving: bfloat16 [8, 256, 4096], P('pipe', 'dp'), may hold values from -2.5 to 2.5
- top_grads: bfloat16 [1, 256, 4096], P(None, 'dp', 'pipe'), may hold values from -2.5 to 2.5
- project_weights: bfloat16 [8, 4096, 384], P('pipe', 'dp'), may hold values from -0.09375 to 0.09375
- output_weights: bfloat16 [8, 4096, 128], P('pipe', 'dp'), may hold values from -0.5 to 0.5
Outputs:
- project_grads: float32 [8, 4096, 384], P('pipe', 'dp')
- output_grads: float32 [8, 4096, 128], P('pipe', 'dp')
- passed_back: bfloat16 [8, 256, 4096], P('pipe', 'dp')
The draws below stay inside these ranges and needn't reach their ends.
All inputs are finite; a program needn't handle non-finite values.
Results may differ from the reference program's by a relative error of at most 0.015.
Values may be sent and summed in bfloat16 or wider, within the bound.
No kernel may reach another device: no remote copies, remote signals or barrier semaphores. Data moves between devices by JAX's collectives and lax.ppermute only.
A program may use at most 64 MiB of HBM per device.

```python
import math
import jax
import jax.numpy as jnp
from jax import lax

D = 4096
HD = 128
SEQ = 64
TICKS = 2
ROWS = 256
N_PIPE = 8
N_DP = 4


def levels(stream_key, shape, split, low, largest):
    def one(dim, parts):
        draws = jax.random.uniform(jax.random.fold_in(jax.random.fold_in(stream_key, 6), dim), (parts,), jnp.float32, low / len(split), largest / len(split))
        return jnp.repeat(jnp.exp(draws), shape[dim] // parts).reshape((-1,) + (1,) * (len(shape) - dim - 1))

    factor_of = one(*split[0])
    for cut in split[1:]:
        factor_of = factor_of * one(*cut)
    return factor_of


def noise(key, dims, scale, reach, shards=(), kind=jnp.bfloat16):
    result = jax.random.normal(key, dims, jnp.float32) * scale
    if len(shards) > 0:
        result = levels(key, dims, shards, -0.22, 0.18) * result
    return jnp.clip(result, min=-reach, max=reach).astype(kind)


def setup_inputs(seed: int = 0) -> dict:
    streams_of = jax.random.split(jax.random.key(seed), 6)
    section_inputs = noise(streams_of[0], (N_PIPE, TICKS, ROWS, D), 1.0, 6.0, ((0, 8), (2, 4)))
    arriving = noise(streams_of[1], (N_PIPE, ROWS, D), 0.25, 2.5, ((0, 8), (1, 4)))
    top_grads = noise(streams_of[2], (TICKS - 1, ROWS, D), 0.25, 2.5, ((1, 4), (2, 8)))
    project_weights = noise(streams_of[3], (N_PIPE, D, 3 * HD), D ** -0.5, 0.09375, ((0, 8), (1, 4)))
    output_weights = noise(streams_of[4], (N_PIPE, D, HD), HD ** -0.5, 0.5, ((0, 8), (1, 4)))
    return dict(section_inputs=section_inputs, arriving=arriving, top_grads=top_grads, project_weights=project_weights, output_weights=output_weights)


EPSILON = 1e-06

def normalize(values):
    centered = values - lax.optimization_barrier(jnp.mean(values, axis=-1, keepdims=True))
    inverse = lax.rsqrt(lax.optimization_barrier(jnp.mean(centered * centered, axis=-1, keepdims=True)) + EPSILON)
    return (centered * inverse, inverse)

def norm_back(gradient, normed, inverse):
    centered = gradient - lax.optimization_barrier(jnp.mean(gradient, axis=-1, keepdims=True))
    return inverse * (centered - normed * lax.optimization_barrier(jnp.mean(gradient * normed, axis=-1, keepdims=True)))

def section_tick(inputs, incoming, project_weights, output_weights):
    head_size = output_weights.shape[1]
    root_size = math.sqrt(head_size)
    normed, inverse = normalize(inputs.astype(jnp.float32))
    hidden = normed.astype(jnp.bfloat16)
    projected = jnp.dot(hidden, project_weights, preferred_element_type=jnp.float32)
    query, query_scale = normalize(projected[:, :head_size])
    key_normed, key_scale = normalize(projected[:, head_size:2 * head_size])
    query_half = query.astype(jnp.bfloat16)
    key_half = key_normed.astype(jnp.bfloat16)
    value_half = projected[:, 2 * head_size:].astype(jnp.bfloat16)
    scores = jnp.dot(query_half, key_half.T, preferred_element_type=jnp.float32) / root_size
    powered = jnp.exp(scores)
    attention = powered / lax.optimization_barrier(jnp.sum(powered, axis=-1, keepdims=True))
    attention_half = attention.astype(jnp.bfloat16)
    mixed_half = jnp.dot(attention_half, value_half, preferred_element_type=jnp.float32).astype(jnp.bfloat16)
    head_grad = jnp.dot(incoming, output_weights, preferred_element_type=jnp.float32).astype(jnp.bfloat16)
    prob_grad = jnp.dot(head_grad, value_half.T, preferred_element_type=jnp.float32)
    value_grad = jnp.dot(attention_half.T, head_grad, preferred_element_type=jnp.float32).astype(jnp.bfloat16)
    score_grad = (attention * (prob_grad - lax.optimization_barrier(jnp.sum(attention * prob_grad, axis=-1, keepdims=True))) / root_size).astype(jnp.bfloat16)
    query_grad = jnp.dot(score_grad, key_half, preferred_element_type=jnp.float32)
    key_grad = jnp.dot(score_grad.T, query_half, preferred_element_type=jnp.float32)
    normed_grads = jnp.concatenate([norm_back(query_grad, query, query_scale), norm_back(key_grad, key_normed, key_scale)], axis=1).astype(jnp.bfloat16)
    proj_grad = jnp.concatenate([normed_grads, value_grad], axis=1)
    hidden_grad = jnp.dot(proj_grad, project_weights.T, preferred_element_type=jnp.float32)
    passed = (incoming.astype(jnp.float32) + norm_back(hidden_grad, normed, inverse)).astype(jnp.bfloat16)
    part_project = jnp.dot(hidden.T, proj_grad, preferred_element_type=jnp.float32)
    part_output = jnp.dot(incoming.T, mixed_half, preferred_element_type=jnp.float32)
    return (passed, part_project, part_output)

def reference(section_inputs, arriving, top_grads, project_weights, output_weights):
    section_count = section_inputs.shape[0]
    tick_count = section_inputs.shape[1]
    width = section_inputs.shape[3]
    project_width = project_weights.shape[2]
    output_width = output_weights.shape[2]
    tick_step = jax.vmap(section_tick)

    def per_replica(totals, replica):
        offset = (replica * SEQ).astype(jnp.int32)
        inputs = lax.dynamic_slice_in_dim(section_inputs, offset, SEQ, 2)
        incoming = lax.dynamic_slice_in_dim(arriving, offset, SEQ, 1)
        later_grads = lax.dynamic_slice_in_dim(top_grads, offset, SEQ, 1)
        sum_project = jnp.zeros((section_count, width, project_width), jnp.float32)
        sum_output = jnp.zeros((section_count, width, output_width), jnp.float32)
        passed = incoming
        for tick_index in range(tick_count):
            passed, part_project, part_output = tick_step(inputs[:, tick_index], incoming, project_weights, output_weights)
            sum_project = sum_project + part_project
            sum_output = sum_output + part_output
            if tick_index + 1 < tick_count:
                incoming = jnp.concatenate([passed[1:], later_grads[tick_index][None]], axis=0)
        rounded_project = lax.optimization_barrier(sum_project.astype(jnp.bfloat16))
        rounded_output = lax.optimization_barrier(sum_output.astype(jnp.bfloat16))
        new_totals = (totals[0] + rounded_project.astype(jnp.float32), totals[1] + rounded_output.astype(jnp.float32))
        return (new_totals, passed)
    start_totals = (jnp.zeros((section_count, width, project_width), jnp.float32), jnp.zeros((section_count, width, output_width), jnp.float32))
    totals, passed_all = lax.scan(per_replica, start_totals, jnp.arange(N_DP, dtype=jnp.int32))
    passed_back = jnp.transpose(passed_all, (1, 0, 2, 3)).reshape(section_count, N_DP * SEQ, width)
    return (totals[0], totals[1], passed_back)
```

```python
import math

import jax
import jax.numpy as jnp
from jax import lax
from jax.sharding import PartitionSpec as P

EPSILON = 1e-06
CONTRACT_FIRST = (((0,), (0,)), ((), ()))
CONTRACT_LAST = (((1,), (1,)), ((), ()))
F32 = jnp.float32
BF16 = jnp.bfloat16


def normalize(values):
    centered = values - jnp.mean(values, axis=-1, keepdims=True)
    inverse = lax.rsqrt(jnp.mean(centered * centered, axis=-1, keepdims=True) + EPSILON)
    return (centered * inverse, inverse)


def norm_back(gradient, normed, inverse):
    centered = gradient - jnp.mean(gradient, axis=-1, keepdims=True)
    return inverse * (centered - normed * jnp.mean(gradient * normed, axis=-1, keepdims=True))


def shift(value, steps):
    count = lax.axis_size("dp")
    if steps % count == 0:
        return value
    return lax.ppermute(value, "dp", [(i, (i + steps) % count) for i in range(count)])


def split_two(value):
    high = value.astype(BF16)
    return high, (value - high.astype(F32)).astype(BF16)


def shards(section_inputs, arriving, top_grads, project_weights, output_weights):
    count = lax.axis_size("dp")
    pipe = lax.axis_size("pipe")
    me = lax.axis_index("dp")
    ticks = section_inputs.shape[1]
    seq = section_inputs.shape[2]
    width = section_inputs.shape[3]
    head = output_weights.shape[2]
    part = width // count
    root = math.sqrt(head)
    others = range(count)
    project, output = project_weights[0], output_weights[0]

    def scatter_features(value):
        return [
            shift(lax.dynamic_slice_in_dim(value, (me + j) % count * part, part, 1), j)
            for j in others
        ]

    def sum_at_owner(pieces):
        return sum(shift(pieces[j], -j).astype(F32) for j in others)

    normed, inverse = normalize(section_inputs[0].astype(F32))
    hidden_rows = normed.astype(BF16)
    hidden = [scatter_features(hidden_rows[0])]
    incoming = scatter_features(arriving[0])
    hidden += [scatter_features(hidden_rows[t]) for t in range(1, ticks)]

    per_owner = pipe // count
    gathered = []
    for j in others:
        pairs = [
            (q * count + (q // per_owner - j) % count, q * count + q // per_owner)
            for q in range(pipe)
        ]
        gathered.append(lax.ppermute(top_grads, ("pipe", "dp"), pairs) if j else top_grads)
    gathered = jnp.stack(gathered)
    top = jnp.concatenate(
        [
            lax.ppermute(
                gathered,
                ("pipe", "dp"),
                [((per_owner * s + a) * count + s, (pipe - 1) * count + s) for s in range(count)],
            )
            for a in range(per_owner)
        ],
        axis=3,
    )

    row_mean = jnp.sum(project.astype(F32), axis=0, keepdims=True) / width
    row_mean = jnp.broadcast_to(row_mean, (16, 3 * head)).astype(BF16)
    row_mean = sum(shift(row_mean, j).astype(F32) for j in others)[:1]

    project_sums = [jnp.zeros((part, 3 * head), F32) for _ in others]
    output_sums = [jnp.zeros((part, head), F32) for _ in others]
    for t in range(ticks):
        mine = [
            jnp.dot(hidden[t][j], project, preferred_element_type=F32).astype(BF16) for j in others
        ]
        heads = [
            jnp.dot(incoming[j], output, preferred_element_type=F32).astype(BF16) for j in others
        ]
        projected = sum_at_owner(mine)
        query, query_scale = normalize(projected[:, :head])
        key, key_scale = normalize(projected[:, head : 2 * head])
        query_half, key_half = query.astype(BF16), key.astype(BF16)
        value_half = projected[:, 2 * head :].astype(BF16)
        scores = lax.dot_general(query_half, key_half, CONTRACT_LAST, preferred_element_type=F32)
        powered = jnp.exp(scores / root)
        attention = powered / jnp.sum(powered, axis=-1, keepdims=True)
        attention_half = attention.astype(BF16)
        mixed = jnp.dot(attention_half, value_half, preferred_element_type=F32).astype(BF16)

        head_grad = sum_at_owner(heads).astype(BF16)
        prob_grad = lax.dot_general(
            head_grad, value_half, CONTRACT_LAST, preferred_element_type=F32
        )
        value_grad = lax.dot_general(
            attention_half, head_grad, CONTRACT_FIRST, preferred_element_type=F32
        ).astype(BF16)
        score_grad = (
            attention
            * (prob_grad - jnp.sum(attention * prob_grad, axis=-1, keepdims=True))
            / root
        ).astype(BF16)
        query_grad = jnp.dot(score_grad, key_half, preferred_element_type=F32)
        key_grad = lax.dot_general(
            score_grad, query_half, CONTRACT_FIRST, preferred_element_type=F32
        )
        proj_grad = jnp.concatenate(
            [
                norm_back(query_grad, query, query_scale).astype(BF16),
                norm_back(key_grad, key, key_scale).astype(BF16),
                value_grad,
            ],
            axis=1,
        )
        wide = proj_grad.astype(F32)
        scale = inverse[t]
        offset = scale * jnp.sum(wide * row_mean, axis=-1, keepdims=True)
        slope = scale * (jnp.sum(wide * projected, axis=-1, keepdims=True) / width)
        facts = [*split_two(scale), *split_two(offset), *split_two(slope)]
        facts.append(jnp.zeros((seq, head - len(facts)), BF16))
        message = jnp.concatenate([proj_grad, mixed, *facts], axis=1)
        messages = [shift(message, j) for j in others]

        passed = []
        for j in others:
            grad = messages[j][:, : 3 * head]
            mix = messages[j][:, 3 * head : 4 * head]
            numbers = messages[j][:, 4 * head :].astype(F32)
            scale, offset, slope = (
                numbers[:, i : i + 1] + numbers[:, i + 1 : i + 2] for i in (0, 2, 4)
            )
            hidden_grad = lax.dot_general(
                grad, project, CONTRACT_LAST, preferred_element_type=F32
            )
            passed.append(
                (
                    incoming[j].astype(F32)
                    + (scale * hidden_grad - offset - slope * hidden[t][j].astype(F32))
                ).astype(BF16)
            )
            project_sums[j] = project_sums[j] + lax.dot_general(
                hidden[t][j], grad, CONTRACT_FIRST, preferred_element_type=F32
            )
            output_sums[j] = output_sums[j] + lax.dot_general(
                incoming[j], mix, CONTRACT_FIRST, preferred_element_type=F32
            )
        if t + 1 < ticks:
            received = lax.ppermute(
                jnp.stack(passed), "pipe", [(p, (p - 1) % pipe) for p in range(pipe)]
            )
            last = lax.axis_index("pipe") == pipe - 1
            received = jnp.where(last, top[:, t], received)
            incoming = [received[j] for j in others]
    back = [shift(passed[j], -j) for j in others]
    passed_back = jnp.zeros((seq, width), BF16)
    for j in others:
        passed_back = lax.dynamic_update_slice_in_dim(
            passed_back, back[j], (me + j) % count * part, 1
        )
    project_grads = sum(value.astype(BF16).astype(F32) for value in project_sums)
    output_grads = sum(value.astype(BF16).astype(F32) for value in output_sums)
    return (project_grads[None], output_grads[None], passed_back[None])


def solution(mesh):
    in_specs = (
        P("pipe", None, "dp", None),
        P("pipe", "dp", None),
        P(None, "dp", "pipe"),
        P("pipe", "dp", None),
        P("pipe", "dp", None),
    )
    out_specs = (P("pipe", "dp", None), P("pipe", "dp", None), P("pipe", "dp", None))
    return jax.shard_map(shards, mesh=mesh, in_specs=in_specs, out_specs=out_specs, check_vma=False)
```

```python
import functools
import math

import jax
import jax.numpy as jnp
from jax import lax
from jax.experimental import pallas as pl
from jax.experimental.pallas import tpu as pltpu
from jax.sharding import PartitionSpec as P

EPSILON = 1e-06
CONTRACT_FIRST = (((0,), (0,)), ((), ()))
CONTRACT_LAST = (((1,), (1,)), ((), ()))
F32 = jnp.float32
BF16 = jnp.bfloat16
ROW_TILE = 16
LANES = 128
BOTH = ("pipe", "dp")


def shape(*dims, kind=BF16):
    return jax.ShapeDtypeStruct(dims, kind)


def kernel_call(body, outs, scalars, arrays, scratch=(), flops=0):
    moved = sum(math.prod(a.shape) * a.dtype.itemsize for a in [*arrays, *outs])
    return pl.pallas_call(
        body,
        out_shape=tuple(outs),
        in_specs=[pl.BlockSpec(memory_space=pltpu.SMEM)] * len(scalars)
        + [pl.BlockSpec(memory_space=pltpu.VMEM)] * len(arrays),
        out_specs=tuple(pl.BlockSpec(memory_space=pltpu.VMEM) for _ in outs),
        scratch_shapes=list(scratch),
        compiler_params=pltpu.CompilerParams(vmem_limit_bytes=24 * 1024 * 1024),
        cost_estimate=pl.CostEstimate(flops=flops, bytes_accessed=moved, transcendentals=0),
    )(*[s.reshape(1).astype(jnp.int32) for s in scalars], *arrays)


def dot(left, right, contract=(((1,), (0,)), ((), ()))):
    return lax.dot_general(left, right, contract, preferred_element_type=F32)


def normalize(values):
    centered = values - jnp.mean(values, axis=-1, keepdims=True)
    inverse = lax.rsqrt(jnp.mean(centered * centered, axis=-1, keepdims=True) + EPSILON)
    return (centered * inverse, inverse)


def norm_back(gradient, normed, inverse):
    centered = gradient - jnp.mean(gradient, axis=-1, keepdims=True)
    return inverse * (centered - normed * jnp.mean(gradient * normed, axis=-1, keepdims=True))


def hidden_pieces(inputs, extra, me, count):
    ticks, seq, width = inputs.shape
    part = width // count
    extras = [] if extra is None else [extra]
    slots = ticks + len(extras)

    def body(me_ref, x_ref, *refs):
        extra_refs, refs = refs[: len(extras)], refs[len(extras) :]
        outs, scale_ref, hidden_ref = refs[:count], refs[count], refs[count + 1]
        for t in range(ticks):
            for row in range(0, seq, ROW_TILE):
                rows = slice(row, row + ROW_TILE)
                normed, inverse = normalize(x_ref[t, rows, :].astype(F32))
                hidden_ref[t, rows, :] = normed.astype(BF16)
                scale_ref[t, rows, :] = jnp.broadcast_to(inverse, (ROW_TILE, LANES))
        for j in range(count):
            owner = lax.rem(me_ref[0] + j, count)
            columns = pl.ds(pl.multiple_of(owner * part, LANES), part)
            for t in range(ticks):
                outs[j][t] = hidden_ref[t, :, columns]
            for extra_ref in extra_refs:
                outs[j][ticks] = extra_ref[:, columns]

    outs = [shape(slots, seq, part) for _ in range(count)]
    outs.append(shape(ticks, seq, LANES, kind=F32))
    result = kernel_call(
        body, outs, [me], [inputs, *extras], [pltpu.VMEM((ticks, seq, width), BF16)]
    )
    return list(result[:count]), result[count]


def first_partials(pieces, project, output, width):
    count = len(pieces)
    seq = pieces[0].shape[1]
    wide, head = project.shape[1], output.shape[1]

    def body(*refs):
        piece_refs, project_ref, output_ref = refs[:count], refs[count], refs[count + 1]
        outs = refs[count + 2 :]
        project, output = project_ref[...], output_ref[...]
        sums = jnp.sum(project.astype(F32), axis=0, keepdims=True) / width
        sums = jnp.broadcast_to(sums, (ROW_TILE, wide)).astype(BF16)
        for j in range(count):
            outs[j][:seq, :wide] = dot(piece_refs[j][0], project).astype(BF16)
            outs[j][:seq, wide:] = dot(piece_refs[j][1], output).astype(BF16)
            outs[j][seq:, :wide] = sums
            outs[j][seq:, wide:] = jnp.zeros((ROW_TILE, head), BF16)

    outs = [shape(seq + ROW_TILE, wide + head) for _ in range(count)]
    return list(kernel_call(body, outs, [], [*pieces, project, output]))


def later_partials(pieces, tick, project):
    count = len(pieces)
    seq = pieces[0].shape[1]
    wide = project.shape[1]

    def body(*refs):
        project = refs[count][...]
        for j in range(count):
            refs[count + 1 + j][...] = dot(refs[j][tick], project).astype(BF16)

    return list(kernel_call(body, [shape(seq, wide)] * count, [], [*pieces, project]))


def split_two(value):
    high = value.astype(BF16).astype(F32)
    return high, value - high


def attention_message(projected_parts, head_parts, mean_parts, scales, tick, width):
    seq = scales.shape[1]
    head = head_parts[0].shape[1]
    lists = (projected_parts, head_parts, mean_parts)
    sizes = [len(part) for part in lists]
    root = math.sqrt(head)
    wide = 3 * head

    def body(*refs):
        refs = list(refs)
        projected, head_grad, row_mean = (
            sum(refs.pop(0)[...].astype(F32) for _ in range(size)) for size in sizes
        )
        scale_ref, out_ref = refs
        query, query_scale = normalize(projected[:, :head])
        key, key_scale = normalize(projected[:, head : 2 * head])
        query_half, key_half = query.astype(BF16), key.astype(BF16)
        value_half = projected[:, 2 * head :].astype(BF16)
        powered = jnp.exp(dot(query_half, key_half, CONTRACT_LAST) / root)
        attention = powered / jnp.sum(powered, axis=-1, keepdims=True)
        attention_half = attention.astype(BF16)
        out_ref[:, wide : wide + head] = dot(attention_half, value_half).astype(BF16)
        head_half = head_grad.astype(BF16)
        prob_grad = dot(head_half, value_half, CONTRACT_LAST)
        value_grad = dot(attention_half, head_half, CONTRACT_FIRST).astype(BF16)
        score_grad = (
            attention
            * (prob_grad - jnp.sum(attention * prob_grad, axis=-1, keepdims=True))
            / root
        ).astype(BF16)
        query_grad = norm_back(dot(score_grad, key_half), query, query_scale).astype(BF16)
        key_grad = norm_back(
            dot(score_grad, query_half, CONTRACT_FIRST), key, key_scale
        ).astype(BF16)
        out_ref[:, :head] = query_grad
        out_ref[:, head : 2 * head] = key_grad
        out_ref[:, 2 * head : wide] = value_grad
        proj_grad = jnp.concatenate([query_grad, key_grad, value_grad], axis=1).astype(F32)
        scale = scale_ref[tick, :, :1]
        offset = scale * jnp.sum(proj_grad * row_mean[:1], axis=-1, keepdims=True)
        slope = scale * (jnp.sum(proj_grad * projected, axis=-1, keepdims=True) / width)
        lane = lax.broadcasted_iota(jnp.int32, (seq, LANES), 1)
        numbers = jnp.zeros((seq, LANES), F32)
        facts = [*split_two(scale), *split_two(offset), *split_two(slope)]
        for place, fact in enumerate(facts):
            numbers = jnp.where(lane == place, fact, numbers)
        out_ref[:, wide + head :] = numbers.astype(BF16)

    arrays = [part for group in lists for part in group]
    return kernel_call(body, [shape(seq, wide + head + LANES)], [], [*arrays, scales])[0]


def input_gradient(message_ref, incoming, hidden, project, wide, head):
    numbers = message_ref[:, wide + head :].astype(F32)
    scale, offset, slope = (numbers[:, i : i + 1] + numbers[:, i + 1 : i + 2] for i in (0, 2, 4))
    hidden_grad = dot(message_ref[:, :wide], project, CONTRACT_LAST)
    change = scale * hidden_grad - offset - slope * hidden.astype(F32)
    return (incoming.astype(F32) + change).astype(BF16)


def middle_step(messages, incoming, inc_slot, hidden, hid_slot, tops, tick, first, project, below):
    count, (_, seq, part) = len(messages), hidden[0].shape
    wide, head = project.shape[1], below.shape[1]
    runs = len(tops)
    run = part // runs

    def body(first_ref, *refs):
        refs = list(refs)
        message_refs, inc_refs, hid_refs = (
            [refs.pop(0) for _ in range(count)] for _ in range(3)
        )
        top_refs = [refs.pop(0) for _ in range(runs)]
        project_ref, below_ref, passed_ref, *head_refs = refs
        is_first = first_ref[0] == 1

        @pl.when(is_first)
        def _():
            for j in range(count):
                for a in range(runs):
                    passed_ref[j, :, a * run : (a + 1) * run] = top_refs[a][j, tick]

        @pl.when(jnp.logical_not(is_first))
        def _():
            for j in range(count):
                passed_ref[j] = input_gradient(
                    message_refs[j],
                    inc_refs[j][inc_slot],
                    hid_refs[j][hid_slot],
                    project_ref[...],
                    wide,
                    head,
                )

        for j in range(count):
            head_refs[j][...] = dot(passed_ref[j], below_ref[...]).astype(BF16)

    outs = [shape(count, seq, part)] + [shape(seq, head)] * count
    arrays = [*messages, *incoming, *hidden, *tops, project, below]
    passed, *heads = kernel_call(body, outs, [first], arrays)
    return passed, heads


def last_step(messages, incoming, hidden, hid_slot, project, head):
    count, (_, seq, part) = len(messages), hidden[0].shape
    wide = project.shape[1]

    def body(*refs):
        incoming_ref, project_ref = refs[2 * count], refs[2 * count + 1]
        for j in range(count):
            refs[2 * count + 2 + j][...] = input_gradient(
                refs[j], incoming_ref[j], refs[count + j][hid_slot], project_ref[...], wide, head
            )

    arrays = [*messages, *hidden, incoming, project]
    return list(kernel_call(body, [shape(seq, part)] * count, [], arrays))


def weight_gradients(hidden, incoming, messages, head):
    ticks, count = len(messages), len(messages[0])
    arrays, places = [], []
    for group in (hidden, incoming):
        for t in range(ticks):
            for j in range(count):
                array, index = group[t][j]
                spots = [i for i, other in enumerate(arrays) if other is array]
                if not spots:
                    arrays.append(array)
                    spots = [len(arrays) - 1]
                places.append((spots[0], index))
    base = len(arrays)
    for t in range(ticks):
        arrays += messages[t]
    seq, part = arrays[0].shape[-2:]
    wide = 3 * head
    block = min(part, 256)

    def body(*refs):
        project_ref, output_ref = refs[len(arrays) :]

        def rows(group, t, j, columns):
            spot, index = places[(group * ticks + t) * count + j]
            return refs[spot][index, :, columns]

        for start in range(0, part, block):
            columns = slice(start, start + block)
            project_sum, output_sum = 0.0, 0.0
            for j in range(count):
                project_part, output_part = 0.0, 0.0
                for t in range(ticks):
                    message = refs[base + t * count + j]
                    project_part += dot(
                        rows(0, t, j, columns), message[:, :wide], CONTRACT_FIRST
                    )
                    output_part += dot(
                        rows(1, t, j, columns), message[:, wide : wide + head], CONTRACT_FIRST
                    )
                project_sum += project_part.astype(BF16).astype(F32)
                output_sum += output_part.astype(BF16).astype(F32)
            project_ref[columns, :] = project_sum
            output_ref[columns, :] = output_sum

    outs = [shape(part, wide, kind=F32), shape(part, head, kind=F32)]
    return kernel_call(body, outs, [], arrays)


def join_features(pieces, me):
    count = len(pieces)
    seq, part = pieces[0].shape

    def body(me_ref, *refs):
        for j in range(count):
            owner = lax.rem(me_ref[0] + j, count)
            columns = pl.ds(pl.multiple_of(owner * part, LANES), part)
            refs[count][:, columns] = refs[j][...]

    return kernel_call(body, [shape(seq, part * count)], [me], pieces)[0]


def shift(value, steps):
    count = lax.axis_size("dp")
    if steps % count == 0:
        return value
    return lax.ppermute(value, "dp", [(i, (i + steps) % count) for i in range(count)])


def down(value, steps=0):
    pipe, count = lax.axis_size("pipe"), lax.axis_size("dp")
    pairs = [
        (p * count + r, (p - 1) % pipe * count + (r + steps) % count)
        for p in range(pipe)
        for r in range(count)
    ]
    return lax.ppermute(value, BOTH, pairs)


def top_to_first(top_grads):
    pipe, count = lax.axis_size("pipe"), lax.axis_size("dp")
    runs = pipe // count
    gathered = [top_grads]
    for j in range(1, count):
        pairs = [(q * count + (q // runs - j) % count, q * count + q // runs) for q in range(pipe)]
        gathered.append(lax.ppermute(top_grads, BOTH, pairs))
    gathered = jnp.stack(gathered)
    return [
        lax.ppermute(gathered, BOTH, [((runs * s + a) * count + s, s) for s in range(count)])
        for a in range(runs)
    ]


def shards(section_inputs, arriving, top_grads, project_weights, output_weights):
    count = lax.axis_size("dp")
    pipe = lax.axis_size("pipe")
    me = lax.axis_index("dp")
    first = lax.axis_index("pipe") == 0
    _, ticks, seq, width = section_inputs.shape
    head = output_weights.shape[2]
    project, output = project_weights[0], output_weights[0]
    others = range(count)

    pieces, first_scale = hidden_pieces(section_inputs[0, :1], arriving[0], me, count)
    first_pieces = [shift(pieces[j], j) for j in others]
    pieces, later_scale = hidden_pieces(section_inputs[0, 1:], None, me, count)
    later_pieces = [shift(pieces[j], j) for j in others]
    below = lax.ppermute(output, "pipe", [(p, (p + 1) % pipe) for p in range(pipe)])
    tops = top_to_first(top_grads)

    partials = first_partials(first_pieces, project, output, width)
    partials = [shift(partials[j], -j) for j in others]
    projected = [value[:seq, : 3 * head] for value in partials]
    heads = [value[:seq, 3 * head :] for value in partials]
    means = [value[seq:, : 3 * head] for value in partials]

    hidden = [[(first_pieces[j], 0) for j in others]]
    incoming = [[(first_pieces[j], 1) for j in others]]
    messages = []
    for t in range(ticks):
        scales, slot = (first_scale, 0) if t == 0 else (later_scale, t - 1)
        message = attention_message(projected, heads, means, scales, slot, width)
        messages.append([shift(message, j) for j in others])
        hidden_now = [array for array, _ in hidden[t]]
        incoming_now = [array for array, _ in incoming[t]]
        if t + 1 < ticks:
            if t > 0:
                incoming_now = [passed[j][None] for j in others]
            passed, heads = middle_step(
                messages[t],
                incoming_now,
                1 if t == 0 else 0,
                hidden_now,
                slot,
                tops,
                t,
                first,
                project,
                below,
            )
            heads = [down(heads[j], -j) for j in others]
            passed = down(passed)
            projected = later_partials(later_pieces, t, project)
            projected = [shift(projected[j], -j) for j in others]
            hidden.append([(later_pieces[j], t) for j in others])
            incoming.append([(passed, j) for j in others])
    back = last_step(messages[-1], passed, hidden_now, slot, project, head)
    back = [shift(back[j], -j) for j in others]
    project_grads, output_grads = weight_gradients(hidden, incoming, messages, head)
    passed_back = join_features(back, me)
    return (project_grads[None], output_grads[None], passed_back[None])


def solution(mesh):
    in_specs = (
        P("pipe", None, "dp", None),
        P("pipe", "dp", None),
        P(None, "dp", "pipe"),
        P("pipe", "dp", None),
        P("pipe", "dp", None),
    )
    out_specs = (P("pipe", "dp", None), P("pipe", "dp", None), P("pipe", "dp", None))
    return jax.shard_map(shards, mesh=mesh, in_specs=in_specs, out_specs=out_specs, check_vma=False)
```

```python
import functools
import math

import jax
import jax.numpy as jnp
from jax import lax
from jax.experimental import pallas as pl
from jax.experimental.pallas import tpu as pltpu
from jax.sharding import PartitionSpec as P

EPSILON = 1e-06
CONTRACT_FIRST = (((0,), (0,)), ((), ()))
CONTRACT_LAST = (((1,), (1,)), ((), ()))
F32 = jnp.float32
BF16 = jnp.bfloat16
ROW_TILE = 16
LANES = 128
BOTH = ("pipe", "dp")


def shape(*dims, kind=BF16):
    return jax.ShapeDtypeStruct(dims, kind)


def kernel_call(body, outs, scalars, arrays, scratch=()):
    return pl.pallas_call(
        body,
        out_shape=tuple(outs),
        in_specs=[pl.BlockSpec(memory_space=pltpu.SMEM)] * len(scalars)
        + [pl.BlockSpec(memory_space=pltpu.VMEM)] * len(arrays),
        out_specs=tuple(pl.BlockSpec(memory_space=pltpu.VMEM) for _ in outs),
        scratch_shapes=list(scratch),
        compiler_params=pltpu.CompilerParams(vmem_limit_bytes=24 * 1024 * 1024),
        cost_estimate=pl.CostEstimate(flops=1, bytes_accessed=1, transcendentals=0),
    )(*[s.reshape(1).astype(jnp.int32) for s in scalars], *arrays)


def dot(left, right, contract=(((1,), (0,)), ((), ()))):
    return lax.dot_general(left, right, contract, preferred_element_type=F32)


def normalize(values):
    centered = values - jnp.mean(values, axis=-1, keepdims=True)
    inverse = lax.rsqrt(jnp.mean(centered * centered, axis=-1, keepdims=True) + EPSILON)
    return (centered * inverse, inverse)


def norm_back(gradient, normed, inverse):
    centered = gradient - jnp.mean(gradient, axis=-1, keepdims=True)
    return inverse * (centered - normed * jnp.mean(gradient * normed, axis=-1, keepdims=True))


def column(row):
    return jnp.broadcast_to(row, (LANES, LANES)).T


def as_row(column):
    seq = column.shape[0]
    if seq < LANES:
        column = jnp.concatenate([column, jnp.zeros((LANES - seq, LANES), F32)], axis=0)
    return column.T[:1]


def split_two(value):
    high = value.astype(BF16).astype(F32)
    return high, value - high


def replica_of(me_ref, j, count):
    return lax.rem(me_ref[0] + count - j, count)


def block_rows(me_ref, j, count, seq):
    block = replica_of(me_ref, j, count) // 2 + (j % 2) * (count // 2)
    return pl.ds(pl.multiple_of(block * seq, seq), seq)


def first_pieces(inputs, arriving, me, count):
    seq, width = arriving.shape
    part = width // count

    def body(me_ref, x_ref, arriving_ref, *refs):
        outs, (scale_ref, hidden_ref) = refs[:count], refs[count:]
        for row in range(0, seq, ROW_TILE):
            rows = slice(row, row + ROW_TILE)
            normed, inverse = normalize(x_ref[0, rows, :].astype(F32))
            hidden_ref[rows, :] = normed.astype(BF16)
            scale_ref[rows, :] = jnp.broadcast_to(inverse, (ROW_TILE, LANES))
        for j in range(count):
            owner = lax.rem(me_ref[0] + j, count)
            columns = pl.ds(pl.multiple_of(owner * part, LANES), part)
            outs[j][0] = hidden_ref[:, columns]
            outs[j][1] = arriving_ref[:, columns]

    outs = [shape(2, seq, part)] * count + [shape(seq, LANES, kind=F32)]
    scratch = [pltpu.VMEM((seq, width), BF16)]
    result = kernel_call(body, outs, [me], [inputs, arriving], scratch)
    return list(result[:count]), result[count]


def later_pieces(inputs, me, count):
    _, seq, width = inputs.shape
    part = width // count

    def body(me_ref, x_ref, *refs):
        outs, (scale_ref, hidden_ref) = refs[:count], refs[count:]
        for row in range(0, seq, ROW_TILE):
            rows = slice(row, row + ROW_TILE)
            normed, inverse = normalize(x_ref[1, rows, :].astype(F32))
            hidden_ref[rows, :] = normed.astype(BF16)
            scale_ref[rows, :] = jnp.broadcast_to(inverse, (ROW_TILE, LANES))
        for j in range(count):
            owner = lax.rem(me_ref[0] + j, count)
            columns = pl.ds(pl.multiple_of(owner * part, LANES), part)
            outs[j][...] = hidden_ref[:, columns]

    outs = [shape(seq, part)] * count + [shape(seq, LANES, kind=F32)]
    scratch = [pltpu.VMEM((seq, width), BF16)]
    result = kernel_call(body, outs, [me], [inputs], scratch)
    return list(result[:count]), result[count]


def first_partials(pieces, scales, project, output, me, width):
    count = len(pieces)
    _, seq, part = pieces[0].shape
    wide, head = project.shape[1], output.shape[1]
    half, ticks = count // 2, len(scales)
    extra = -(-2 * ticks * half // ROW_TILE) * ROW_TILE

    def body(me_ref, *refs):
        piece_refs, refs = refs[:count], refs[count:]
        scale_refs, (project_ref, output_ref, *outs) = refs[:ticks], refs[ticks:]
        project = project_ref[...]
        for j in range(count):
            out_ref, rows = outs[j % 2], half_rows(me_ref, j, count, seq)
            out_ref[rows, :wide] = dot(piece_refs[j][0], project).astype(BF16)
            out_ref[rows, wide:] = dot(piece_refs[j][1], output_ref[...]).astype(BF16)
        sums = jnp.sum(project.astype(F32), axis=0, keepdims=True) / width
        place = lax.broadcasted_iota(jnp.int32, (extra, LANES), 0) - 2 * ticks * (me_ref[0] // 2)
        facts = jnp.zeros((extra, LANES), F32)
        for t in range(ticks):
            for index, value in enumerate(split_two(as_row(scale_refs[t][...]))):
                facts = jnp.where(place == 2 * t + index, value, facts)
        for out_ref, lanes in zip(outs, (facts, jnp.zeros((extra, LANES), F32))):
            out_ref[half * seq :, :LANES] = lanes.astype(BF16)
            out_ref[half * seq :, LANES:] = jnp.broadcast_to(sums, (extra, wide)).astype(BF16)

    outs = [shape(half * seq + extra, wide + head)] * 2
    return kernel_call(body, outs, [me], [*pieces, *scales, project, output])


def half_rows(me_ref, j, count, seq):
    block = replica_of(me_ref, j, count) // 2
    return pl.ds(pl.multiple_of(block * seq, seq), seq)


def later_partials(pieces, project, me):
    count = len(pieces)
    seq = pieces[0].shape[0]
    wide = project.shape[1]

    def body(me_ref, *refs):
        piece_refs, (project_ref, *outs) = refs[:count], refs[count:]
        for j in range(count):
            value = dot(piece_refs[j][...], project_ref[...])
            outs[j % 2][half_rows(me_ref, j, count, seq), :] = value.astype(BF16)

    return kernel_call(body, [shape(count // 2 * seq, wide)] * 2, [me], [*pieces, project])


def add_two(left, right):
    def body(left_ref, right_ref, out_ref):
        out_ref[...] = (left_ref[...].astype(F32) + right_ref[...].astype(F32)).astype(BF16)

    return kernel_call(body, [shape(*left.shape)], [], [left, right])[0]


def attention_back(projected, head_half, row_mean, scale, seq, outs, width):
    grad_ref, mixed_ref, numbers_ref = outs
    rows, head = head_half.shape
    count = rows // seq
    root = math.sqrt(head)
    query, query_scale = normalize(projected[:, :head])
    key, key_scale = normalize(projected[:, head : 2 * head])
    query_half, key_half = query.astype(BF16), key.astype(BF16)
    value_half = projected[:, 2 * head :].astype(BF16)

    def each(function, *values):
        return jnp.concatenate(
            [function(*(v[r * seq : (r + 1) * seq] for v in values)) for r in range(count)], axis=0
        )

    def last(left, right):
        return dot(left, right, CONTRACT_LAST)

    def leading(left, right):
        return dot(left, right, CONTRACT_FIRST)

    powered = jnp.exp(each(last, query_half, key_half) / root)
    attention = powered / jnp.sum(powered, axis=-1, keepdims=True)
    attention_half = attention.astype(BF16)
    mixed_ref[...] = each(dot, attention_half, value_half).astype(BF16)
    prob_grad = each(last, head_half, value_half)
    value_grad = each(leading, attention_half, head_half).astype(BF16)
    score_grad = (
        attention * (prob_grad - jnp.sum(attention * prob_grad, axis=-1, keepdims=True)) / root
    ).astype(BF16)
    query_grad = norm_back(each(dot, score_grad, key_half), query, query_scale)
    key_grad = norm_back(each(leading, score_grad, query_half), key, key_scale)
    proj_grad = jnp.concatenate(
        [query_grad.astype(BF16), key_grad.astype(BF16), value_grad], axis=1
    )
    grad_ref[...] = proj_grad
    spread = proj_grad.astype(F32)
    offset = scale * jnp.sum(spread * row_mean, axis=-1, keepdims=True)
    slope = scale * (jnp.sum(spread * projected, axis=-1, keepdims=True) / width)
    lane = lax.broadcasted_iota(jnp.int32, (rows, LANES), 1)
    numbers_ref[...] = jnp.where(lane == 0, scale, jnp.where(lane == 1, offset, slope))


def all_rows(half_refs, seq, half, columns):
    return jnp.concatenate([ref[: half * seq, columns] for ref in half_refs], axis=0).astype(F32)


def scale_column(half_refs, tick, ticks, seq, half):
    columns = []
    for ref in half_refs:
        facts = ref[half * seq :, :LANES].astype(F32)
        for block in range(half):
            row = 2 * (ticks * block + tick)
            columns.append(column(facts[row : row + 1] + facts[row + 1 : row + 2])[:seq, :1])
    return jnp.concatenate(columns, axis=0)


def attention_outs(rows, head):
    return [shape(rows, 3 * head), shape(rows, head), shape(rows, LANES, kind=F32)]


def first_attention(halves, seq, half, head, ticks, width):
    rows, wide = 2 * half * seq, 3 * head

    def body(*refs):
        mine = refs[:2]
        attention_back(
            all_rows(mine, seq, half, slice(0, wide)),
            all_rows(mine, seq, half, slice(wide, wide + head)).astype(BF16),
            refs[0][half * seq :, LANES:].astype(F32)[:1],
            scale_column(mine, 0, ticks, seq, half),
            seq,
            refs[2:],
            width,
        )

    return kernel_call(body, attention_outs(rows, head), [], halves)


def later_attention(halves, facts, heads, received, seq, half, head, ticks, me, width):
    rows, count = 2 * half * seq, 2 * half
    part = received.shape[2] - head

    def body(me_ref, *refs):
        mine, facts, refs = refs[:2], refs[2:4], refs[4:]
        head_refs, (received_ref, *outs) = refs[: len(heads)], refs[len(heads) :]
        blocks = []
        for parity in range(2):
            for block in range(half):
                replica = 2 * block + lax.rem(me_ref[0] + parity, 2)
                place = pl.ds(pl.multiple_of(replica * seq, seq), seq)
                total = sum(ref[place, :].astype(F32) for ref in head_refs)
                piece = lax.rem(me_ref[0] + count - replica, count)
                blocks.append(total + received_ref[piece, :, part:].astype(F32))
        attention_back(
            all_rows(mine, seq, half, slice(None)),
            jnp.concatenate(blocks, axis=0).astype(BF16),
            facts[0][half * seq :, LANES:].astype(F32)[:1],
            scale_column(facts, 1, ticks, seq, half),
            seq,
            outs,
            width,
        )

    arrays = [*halves, *facts, *heads, received]
    return kernel_call(body, attention_outs(rows, head), [me], arrays)


def input_gradient(grad, numbers, incoming, hidden, project):
    scale, offset, slope = (numbers[:, i : i + 1] for i in range(3))
    hidden_grad = dot(grad, project, CONTRACT_LAST)
    change = scale * hidden_grad - offset - slope * hidden.astype(F32)
    return (incoming.astype(F32) + change).astype(BF16)


def middle_step(grads, pieces, tops, project, below, me, first):
    count, (_, seq, part) = len(pieces), pieces[0].shape
    head, runs = below.shape[1], len(tops)
    run = part // runs

    def body(me_ref, first_ref, *refs):
        refs = list(refs)
        piece_refs = [refs.pop(0) for _ in range(count)]
        top_refs = [refs.pop(0) for _ in range(runs)]
        grad_ref, numbers_ref, project_ref, below_ref, passed_ref, head_ref = refs
        is_first = first_ref[0] == 1

        @pl.when(is_first)
        def _():
            for j in range(count):
                block = lax.bitwise_xor(me_ref[0], replica_of(me_ref, j, count))
                for a in range(runs):
                    passed_ref[j, :, a * run : (a + 1) * run] = top_refs[a][block]

        @pl.when(jnp.logical_not(is_first))
        def _():
            for j in range(count):
                rows = block_rows(me_ref, j, count, seq)
                hidden, incoming = piece_refs[j][0], piece_refs[j][1]
                passed_ref[j, :, :part] = input_gradient(
                    grad_ref[rows, :], numbers_ref[rows, :], incoming, hidden, project_ref[...]
                )

        for j in range(count):
            value = dot(passed_ref[j, :, :part], below_ref[...]).astype(BF16)
            passed_ref[j, :, part:] = value
            replica = replica_of(me_ref, j, count)
            head_ref[pl.ds(pl.multiple_of(replica * seq, seq), seq), :] = value

    outs = [shape(count, seq, part + head), shape(count * seq, head)]
    return kernel_call(body, outs, [me, first], [*pieces, *tops, *grads, project, below])


def last_step(grads, received, pieces, project, me):
    count, (seq, part) = len(pieces), pieces[0].shape

    def body(me_ref, *refs):
        piece_refs, (grad_ref, numbers_ref, received_ref, project_ref, *outs) = (
            refs[:count],
            refs[count:],
        )
        for j in range(count):
            rows = block_rows(me_ref, j, count, seq)
            outs[j][...] = input_gradient(
                grad_ref[rows, :],
                numbers_ref[rows, :],
                received_ref[j, :, :part],
                piece_refs[j][...],
                project_ref[...],
            )

    arrays = [*pieces, *grads, received, project]
    return list(kernel_call(body, [shape(seq, part)] * count, [me], arrays))


def weight_gradients(pieces, later, received, first_grads, later_grads, me):
    count, (_, seq, part) = len(pieces), pieces[0].shape
    wide, head = first_grads[0].shape[1], first_grads[1].shape[1]
    block = min(part, 256)

    def body(me_ref, *refs):
        piece_refs, later_refs, refs = refs[:count], refs[count : 2 * count], refs[2 * count :]
        received_ref, grad0, mixed0, grad1, mixed1, project_ref, output_ref = refs
        for start in range(0, part, block):
            columns = slice(start, start + block)
            project_sum, output_sum = 0.0, 0.0
            for j in range(count):
                rows = block_rows(me_ref, j, count, seq)
                value = dot(piece_refs[j][0, :, columns], grad0[rows, :], CONTRACT_FIRST)
                value += dot(later_refs[j][:, columns], grad1[rows, :], CONTRACT_FIRST)
                project_sum += value.astype(BF16).astype(F32)
                value = dot(piece_refs[j][1, :, columns], mixed0[rows, :], CONTRACT_FIRST)
                value += dot(received_ref[j, :, columns], mixed1[rows, :], CONTRACT_FIRST)
                output_sum += value.astype(BF16).astype(F32)
            project_ref[columns, :] = project_sum
            output_ref[columns, :] = output_sum

    outs = [shape(part, wide, kind=F32), shape(part, head, kind=F32)]
    arrays = [*pieces, *later, received, *first_grads, *later_grads]
    return kernel_call(body, outs, [me], arrays)


def join_features(pieces, me):
    count = len(pieces)
    seq, part = pieces[0].shape

    def body(me_ref, *refs):
        for j in range(count):
            owner = lax.rem(me_ref[0] + j, count)
            columns = pl.ds(pl.multiple_of(owner * part, LANES), part)
            refs[count][:, columns] = refs[j][...]

    return kernel_call(body, [shape(seq, part * count)], [me], pieces)[0]


def shift(value, steps):
    count = lax.axis_size("dp")
    if steps % count == 0:
        return value
    return lax.ppermute(value, "dp", [(i, (i + steps) % count) for i in range(count)])


def after(value, *earlier):
    return lax.optimization_barrier((value, *earlier))[0]


def down(value, steps=0):
    pipe, count = lax.axis_size("pipe"), lax.axis_size("dp")
    pairs = [
        (p * count + r, (p - 1) % pipe * count + (r + steps) % count)
        for p in range(pipe)
        for r in range(count)
    ]
    return lax.ppermute(value, BOTH, pairs)


def join_pieces(left, right):
    size = left.shape[0]

    def body(left_ref, right_ref, out_ref):
        out_ref[:size] = left_ref[...]
        out_ref[size:] = right_ref[...]

    outs = [shape(2 * size, *left.shape[1:])]
    return kernel_call(body, outs, [], [left, right])[0]


def toward_owner(blocks, bit):
    pipe, count = lax.axis_size("pipe"), lax.axis_size("dp")
    runs = pipe // count
    pairs = [
        (q * count + r, q * count + (r ^ bit))
        for q in range(pipe)
        for r in range(count)
        if (r ^ (q // runs)) % (2 * bit) == bit
    ]
    return lax.ppermute(blocks, BOTH, pairs)


def owner_to_first(blocks, run):
    pipe, count = lax.axis_size("pipe"), lax.axis_size("dp")
    runs = pipe // count
    return lax.ppermute(blocks, BOTH, [((runs * s + run) * count + s, s) for s in range(count)])


def exchanged(value, step):
    count = lax.axis_size("dp")
    return lax.ppermute(value, "dp", [(i, i ^ step) for i in range(count)])


def shards(section_inputs, arriving, top_grads, project_weights, output_weights):
    count = lax.axis_size("dp")
    pipe = lax.axis_size("pipe")
    me = lax.axis_index("dp")
    first = lax.axis_index("pipe") == 0
    _, ticks, seq, width = section_inputs.shape
    head = output_weights.shape[2]
    project, output = project_weights[0], output_weights[0]
    others, half = range(count), count // 2

    blocks, moved = top_grads, toward_owner(top_grads, 1)
    sent, scale = first_pieces(section_inputs[0], arriving[0], me, count)
    pieces = [shift(sent[j], j) for j in others]
    later_sent, later_scale = later_pieces(section_inputs[0], me, count)
    blocks = join_pieces(after(blocks, later_scale), moved)
    bit = 2
    while bit < count // 2:
        blocks = join_pieces(blocks, toward_owner(blocks, bit))
        bit *= 2
    moved = toward_owner(blocks, bit) if bit < count else None

    mine, other = first_partials(
        pieces, [scale, later_scale], after(project, blocks), output, me, width
    )
    below = lax.ppermute(
        after(output, other), "pipe", [(p, (p + 1) % pipe) for p in range(pipe)]
    )
    later_sent = after(tuple(later_sent), other)
    later = [shift(later_sent[j], j) for j in others]
    later_mine, later_other = later_partials(later, project, me)
    total = add_two(after(mine, later_other, below), exchanged(other, 1))
    if moved is not None:
        blocks = join_pieces(after(blocks, total), moved)
    tops = [owner_to_first(blocks, run) for run in range(pipe // count)]
    later_total = add_two(after(later_mine, total), exchanged(later_other, 1))
    step = 2
    while step < count:
        received = exchanged(total, step)
        total = add_two(after(total, later_total), received)
        step *= 2
    halves = [total, exchanged(total, 1)]
    step = 2
    while step < count:
        received = exchanged(later_total, step)
        later_total = add_two(after(later_total, total), received)
        step *= 2
    halves[0] = after(halves[0], later_total)
    later_halves = [later_total, exchanged(later_total, 1)]

    first_grads = first_attention(halves, seq, half, head, ticks, width)
    passed, heads = middle_step(
        [first_grads[0], first_grads[2]], pieces, tops, project, below, me, first
    )
    heads = [down(heads, j) for j in others[1:]]
    received = down(passed)
    later_grads = later_attention(
        later_halves, halves, heads, received, seq, half, head, ticks, me, width
    )
    back = last_step([later_grads[0], later_grads[2]], received, later, project, me)
    mixed = after(later_grads[1], back[0])
    back = [shift(back[j], -j) for j in others]
    project_grads, output_grads = weight_gradients(
        pieces, later, received, first_grads[:2], [later_grads[0], mixed], me
    )
    passed_back = join_features(back, me)
    return (project_grads[None], output_grads[None], passed_back[None])


def solution(mesh):
    in_specs = (
        P("pipe", None, "dp", None),
        P("pipe", "dp", None),
        P(None, "dp", "pipe"),
        P("pipe", "dp", None),
        P("pipe", "dp", None),
    )
    out_specs = (P("pipe", "dp", None), P("pipe", "dp", None), P("pipe", "dp", None))
    return jax.shard_map(shards, mesh=mesh, in_specs=in_specs, out_specs=out_specs, check_vma=False)
```

```python
import functools
import math

import jax
import jax.numpy as jnp
from jax import lax
from jax.experimental import pallas as pl
from jax.experimental.pallas import tpu as pltpu
from jax.sharding import PartitionSpec as P

EPSILON = 1e-06
CONTRACT_FIRST = (((0,), (0,)), ((), ()))
CONTRACT_LAST = (((1,), (1,)), ((), ()))
F32 = jnp.float32
BF16 = jnp.bfloat16
ROW_TILE = 16
LANES = 128
BOTH = ("pipe", "dp")


def shape(*dims, kind=BF16):
    return jax.ShapeDtypeStruct(dims, kind)


def kernel_call(body, outs, scalars, arrays, scratch=()):
    return pl.pallas_call(
        body,
        out_shape=tuple(outs),
        in_specs=[pl.BlockSpec(memory_space=pltpu.SMEM)] * len(scalars)
        + [pl.BlockSpec(memory_space=pltpu.VMEM)] * len(arrays),
        out_specs=tuple(pl.BlockSpec(memory_space=pltpu.VMEM) for _ in outs),
        scratch_shapes=list(scratch),
        compiler_params=pltpu.CompilerParams(vmem_limit_bytes=24 * 1024 * 1024),
        cost_estimate=pl.CostEstimate(flops=1, bytes_accessed=1, transcendentals=0),
    )(*[s.reshape(1).astype(jnp.int32) for s in scalars], *arrays)


def dot(left, right, contract=(((1,), (0,)), ((), ()))):
    return lax.dot_general(left, right, contract, preferred_element_type=F32)


def normalize(values):
    centered = values - jnp.mean(values, axis=-1, keepdims=True)
    inverse = lax.rsqrt(jnp.mean(centered * centered, axis=-1, keepdims=True) + EPSILON)
    return (centered * inverse, inverse)


def norm_back(gradient, normed, inverse):
    centered = gradient - jnp.mean(gradient, axis=-1, keepdims=True)
    return inverse * (centered - normed * jnp.mean(gradient * normed, axis=-1, keepdims=True))


def column(row):
    return jnp.broadcast_to(row, (LANES, LANES)).T


def as_row(column):
    seq = column.shape[0]
    if seq < LANES:
        column = jnp.concatenate([column, jnp.zeros((LANES - seq, LANES), F32)], axis=0)
    return column.T[:1]


def split_two(value):
    high = value.astype(BF16).astype(F32)
    return high, value - high


def replica_of(me_ref, j, count):
    return lax.rem(me_ref[0] + count - j, count)


def block_rows(me_ref, j, count, seq):
    block = replica_of(me_ref, j, count) // 2 + (j % 2) * (count // 2)
    return pl.ds(pl.multiple_of(block * seq, seq), seq)


def first_pieces(inputs, arriving, me, count):
    seq, width = arriving.shape
    part = width // count

    def body(me_ref, x_ref, arriving_ref, *refs):
        outs, (scale_ref, hidden_ref) = refs[:count], refs[count:]
        for row in range(0, seq, ROW_TILE):
            rows = slice(row, row + ROW_TILE)
            normed, inverse = normalize(x_ref[0, rows, :].astype(F32))
            hidden_ref[rows, :] = normed.astype(BF16)
            scale_ref[rows, :] = jnp.broadcast_to(inverse, (ROW_TILE, LANES))
        for j in range(count):
            owner = lax.rem(me_ref[0] + j, count)
            columns = pl.ds(pl.multiple_of(owner * part, LANES), part)
            outs[j][0] = hidden_ref[:, columns]
            outs[j][1] = arriving_ref[:, columns]

    outs = [shape(2, seq, part)] * count + [shape(seq, LANES, kind=F32)]
    scratch = [pltpu.VMEM((seq, width), BF16)]
    result = kernel_call(body, outs, [me], [inputs, arriving], scratch)
    return list(result[:count]), result[count]


def later_pieces(inputs, me, count):
    _, seq, width = inputs.shape
    part = width // count

    def body(me_ref, x_ref, *refs):
        outs, (scale_ref, hidden_ref) = refs[:count], refs[count:]
        for row in range(0, seq, ROW_TILE):
            rows = slice(row, row + ROW_TILE)
            normed, inverse = normalize(x_ref[1, rows, :].astype(F32))
            hidden_ref[rows, :] = normed.astype(BF16)
            scale_ref[rows, :] = jnp.broadcast_to(inverse, (ROW_TILE, LANES))
        for j in range(count):
            owner = lax.rem(me_ref[0] + j, count)
            columns = pl.ds(pl.multiple_of(owner * part, LANES), part)
            outs[j][...] = hidden_ref[:, columns]

    outs = [shape(seq, part)] * count + [shape(seq, LANES, kind=F32)]
    scratch = [pltpu.VMEM((seq, width), BF16)]
    result = kernel_call(body, outs, [me], [inputs], scratch)
    return list(result[:count]), result[count]


def first_partials(pieces, scales, project, output, me, width):
    count = len(pieces)
    _, seq, part = pieces[0].shape
    wide, head = project.shape[1], output.shape[1]
    half, ticks = count // 2, len(scales)
    extra = -(-2 * ticks * half // ROW_TILE) * ROW_TILE

    def body(me_ref, *refs):
        piece_refs, refs = refs[:count], refs[count:]
        scale_refs, (project_ref, output_ref, *outs) = refs[:ticks], refs[ticks:]
        project = project_ref[...]
        for j in range(count):
            out_ref, rows = outs[j % 2], half_rows(me_ref, j, count, seq)
            out_ref[rows, :wide] = dot(piece_refs[j][0], project).astype(BF16)
            out_ref[rows, wide:] = dot(piece_refs[j][1], output_ref[...]).astype(BF16)
        sums = jnp.sum(project.astype(F32), axis=0, keepdims=True) / width
        place = lax.broadcasted_iota(jnp.int32, (extra, LANES), 0) - 2 * ticks * (me_ref[0] // 2)
        facts = jnp.zeros((extra, LANES), F32)
        for t in range(ticks):
            for index, value in enumerate(split_two(as_row(scale_refs[t][...]))):
                facts = jnp.where(place == 2 * t + index, value, facts)
        for out_ref, lanes in zip(outs, (facts, jnp.zeros((extra, LANES), F32))):
            out_ref[half * seq :, :LANES] = lanes.astype(BF16)
            out_ref[half * seq :, LANES:] = jnp.broadcast_to(sums, (extra, wide)).astype(BF16)

    outs = [shape(half * seq + extra, wide + head)] * 2
    return kernel_call(body, outs, [me], [*pieces, *scales, project, output])


def half_rows(me_ref, j, count, seq):
    block = replica_of(me_ref, j, count) // 2
    return pl.ds(pl.multiple_of(block * seq, seq), seq)


def later_partials(pieces, project, me):
    count = len(pieces)
    seq = pieces[0].shape[0]
    wide = project.shape[1]

    def body(me_ref, *refs):
        piece_refs, (project_ref, *outs) = refs[:count], refs[count:]
        for j in range(count):
            value = dot(piece_refs[j][...], project_ref[...])
            outs[j % 2][half_rows(me_ref, j, count, seq), :] = value.astype(BF16)

    return kernel_call(body, [shape(count // 2 * seq, wide)] * 2, [me], [*pieces, project])


def add_two(left, right):
    def body(left_ref, right_ref, out_ref):
        out_ref[...] = (left_ref[...].astype(F32) + right_ref[...].astype(F32)).astype(BF16)

    return kernel_call(body, [shape(*left.shape)], [], [left, right])[0]


def attention_back(projected, head_half, row_mean, scale, seq, outs, width):
    grad_ref, mixed_ref, numbers_ref = outs
    rows, head = head_half.shape
    count = rows // seq
    root = math.sqrt(head)
    query, query_scale = normalize(projected[:, :head])
    key, key_scale = normalize(projected[:, head : 2 * head])
    query_half, key_half = query.astype(BF16), key.astype(BF16)
    value_half = projected[:, 2 * head :].astype(BF16)

    def each(function, *values):
        return jnp.concatenate(
            [function(*(v[r * seq : (r + 1) * seq] for v in values)) for r in range(count)], axis=0
        )

    def last(left, right):
        return dot(left, right, CONTRACT_LAST)

    def leading(left, right):
        return dot(left, right, CONTRACT_FIRST)

    powered = jnp.exp(each(last, query_half, key_half) / root)
    attention = powered / jnp.sum(powered, axis=-1, keepdims=True)
    attention_half = attention.astype(BF16)
    mixed_ref[...] = each(dot, attention_half, value_half).astype(BF16)
    prob_grad = each(last, head_half, value_half)
    value_grad = each(leading, attention_half, head_half).astype(BF16)
    score_grad = (
        attention * (prob_grad - jnp.sum(attention * prob_grad, axis=-1, keepdims=True)) / root
    ).astype(BF16)
    query_grad = norm_back(each(dot, score_grad, key_half), query, query_scale)
    key_grad = norm_back(each(leading, score_grad, query_half), key, key_scale)
    proj_grad = jnp.concatenate(
        [query_grad.astype(BF16), key_grad.astype(BF16), value_grad], axis=1
    )
    grad_ref[...] = proj_grad
    spread = proj_grad.astype(F32)
    offset = scale * jnp.sum(spread * row_mean, axis=-1, keepdims=True)
    slope = scale * (jnp.sum(spread * projected, axis=-1, keepdims=True) / width)
    lane = lax.broadcasted_iota(jnp.int32, (rows, LANES), 1)
    numbers_ref[...] = jnp.where(lane == 0, scale, jnp.where(lane == 1, offset, slope))


def all_rows(half_refs, seq, half, columns):
    return jnp.concatenate([ref[: half * seq, columns] for ref in half_refs], axis=0).astype(F32)


def scale_column(half_refs, tick, ticks, seq, half):
    columns = []
    for ref in half_refs:
        facts = ref[half * seq :, :LANES].astype(F32)
        for block in range(half):
            row = 2 * (ticks * block + tick)
            columns.append(column(facts[row : row + 1] + facts[row + 1 : row + 2])[:seq, :1])
    return jnp.concatenate(columns, axis=0)


def attention_outs(rows, head):
    return [shape(rows, 3 * head), shape(rows, head), shape(rows, LANES, kind=F32)]


def first_attention(halves, seq, half, head, ticks, width):
    rows, wide = 2 * half * seq, 3 * head

    def body(*refs):
        mine = refs[:2]
        attention_back(
            all_rows(mine, seq, half, slice(0, wide)),
            all_rows(mine, seq, half, slice(wide, wide + head)).astype(BF16),
            refs[0][half * seq :, LANES:].astype(F32)[:1],
            scale_column(mine, 0, ticks, seq, half),
            seq,
            refs[2:],
            width,
        )

    return kernel_call(body, attention_outs(rows, head), [], halves)


def later_attention(halves, facts, heads, received, seq, half, head, ticks, me, width):
    rows, count = 2 * half * seq, 2 * half
    part = received.shape[2] - head

    def body(me_ref, *refs):
        mine, facts, refs = refs[:2], refs[2:4], refs[4:]
        head_refs, (received_ref, *outs) = refs[: len(heads)], refs[len(heads) :]
        blocks = []
        for parity in range(2):
            for block in range(half):
                replica = 2 * block + lax.rem(me_ref[0] + parity, 2)
                place = pl.ds(pl.multiple_of(replica * seq, seq), seq)
                total = sum(ref[place, :].astype(F32) for ref in head_refs)
                piece = lax.rem(me_ref[0] + count - replica, count)
                blocks.append(total + received_ref[piece, :, part:].astype(F32))
        attention_back(
            all_rows(mine, seq, half, slice(None)),
            jnp.concatenate(blocks, axis=0).astype(BF16),
            facts[0][half * seq :, LANES:].astype(F32)[:1],
            scale_column(facts, 1, ticks, seq, half),
            seq,
            outs,
            width,
        )

    arrays = [*halves, *facts, *heads, received]
    return kernel_call(body, attention_outs(rows, head), [me], arrays)


def input_gradient(grad, numbers, incoming, hidden, project):
    scale, offset, slope = (numbers[:, i : i + 1] for i in range(3))
    hidden_grad = dot(grad, project, CONTRACT_LAST)
    change = scale * hidden_grad - offset - slope * hidden.astype(F32)
    return (incoming.astype(F32) + change).astype(BF16)


def middle_step(grads, pieces, tops, project, below, me, first):
    count, (_, seq, part) = len(pieces), pieces[0].shape
    head, runs = below.shape[1], len(tops)
    run = part // runs

    def body(me_ref, first_ref, *refs):
        refs = list(refs)
        piece_refs = [refs.pop(0) for _ in range(count)]
        top_refs = [refs.pop(0) for _ in range(runs)]
        grad_ref, numbers_ref, project_ref, below_ref, passed_ref, head_ref = refs
        is_first = first_ref[0] == 1

        @pl.when(is_first)
        def _():
            for j in range(count):
                block = lax.bitwise_xor(me_ref[0], replica_of(me_ref, j, count))
                for a in range(runs):
                    passed_ref[j, :, a * run : (a + 1) * run] = top_refs[a][block]

        @pl.when(jnp.logical_not(is_first))
        def _():
            for j in range(count):
                rows = block_rows(me_ref, j, count, seq)
                hidden, incoming = piece_refs[j][0], piece_refs[j][1]
                passed_ref[j, :, :part] = input_gradient(
                    grad_ref[rows, :], numbers_ref[rows, :], incoming, hidden, project_ref[...]
                )

        for j in range(count):
            value = dot(passed_ref[j, :, :part], below_ref[...]).astype(BF16)
            passed_ref[j, :, part:] = value
            replica = replica_of(me_ref, j, count)
            head_ref[pl.ds(pl.multiple_of(replica * seq, seq), seq), :] = value

    outs = [shape(count, seq, part + head), shape(count * seq, head)]
    return kernel_call(body, outs, [me, first], [*pieces, *tops, *grads, project, below])


def last_step(grads, received, pieces, project, me):
    count, (seq, part) = len(pieces), pieces[0].shape

    def body(me_ref, *refs):
        piece_refs, (grad_ref, numbers_ref, received_ref, project_ref, *outs) = (
            refs[:count],
            refs[count:],
        )
        for j in range(count):
            rows = block_rows(me_ref, j, count, seq)
            outs[j][...] = input_gradient(
                grad_ref[rows, :],
                numbers_ref[rows, :],
                received_ref[j, :, :part],
                piece_refs[j][...],
                project_ref[...],
            )

    arrays = [*pieces, *grads, received, project]
    return list(kernel_call(body, [shape(seq, part)] * count, [me], arrays))


def weight_gradients(pieces, later, received, first_grads, later_grads, me):
    count, (_, seq, part) = len(pieces), pieces[0].shape
    wide, head = first_grads[0].shape[1], first_grads[1].shape[1]
    block = min(part, 256)

    def body(me_ref, *refs):
        piece_refs, later_refs, refs = refs[:count], refs[count : 2 * count], refs[2 * count :]
        received_ref, grad0, mixed0, grad1, mixed1, project_ref, output_ref = refs
        for start in range(0, part, block):
            columns = slice(start, start + block)
            project_sum, output_sum = 0.0, 0.0
            for j in range(count):
                rows = block_rows(me_ref, j, count, seq)
                value = dot(piece_refs[j][0, :, columns], grad0[rows, :], CONTRACT_FIRST)
                value += dot(later_refs[j][:, columns], grad1[rows, :], CONTRACT_FIRST)
                project_sum += value.astype(BF16).astype(F32)
                value = dot(piece_refs[j][1, :, columns], mixed0[rows, :], CONTRACT_FIRST)
                value += dot(received_ref[j, :, columns], mixed1[rows, :], CONTRACT_FIRST)
                output_sum += value.astype(BF16).astype(F32)
            project_ref[columns, :] = project_sum
            output_ref[columns, :] = output_sum

    outs = [shape(part, wide, kind=F32), shape(part, head, kind=F32)]
    arrays = [*pieces, *later, received, *first_grads, *later_grads]
    return kernel_call(body, outs, [me], arrays)


def join_features(pieces, me):
    count = len(pieces)
    seq, part = pieces[0].shape

    def body(me_ref, *refs):
        for j in range(count):
            owner = lax.rem(me_ref[0] + j, count)
            columns = pl.ds(pl.multiple_of(owner * part, LANES), part)
            refs[count][:, columns] = refs[j][...]

    return kernel_call(body, [shape(seq, part * count)], [me], pieces)[0]


def shift(value, steps):
    count = lax.axis_size("dp")
    if steps % count == 0:
        return value
    return lax.ppermute(value, "dp", [(i, (i + steps) % count) for i in range(count)])


def after(value, *earlier):
    return lax.optimization_barrier((value, *earlier))[0]


def down(value, steps=0):
    pipe, count = lax.axis_size("pipe"), lax.axis_size("dp")
    pairs = [
        (p * count + r, (p - 1) % pipe * count + (r + steps) % count)
        for p in range(pipe)
        for r in range(count)
    ]
    return lax.ppermute(value, BOTH, pairs)


def join_pieces(left, right):
    size = left.shape[0]

    def body(left_ref, right_ref, out_ref):
        out_ref[:size] = left_ref[...]
        out_ref[size:] = right_ref[...]

    outs = [shape(2 * size, *left.shape[1:])]
    return kernel_call(body, outs, [], [left, right])[0]


def toward_owner(blocks, bit):
    pipe, count = lax.axis_size("pipe"), lax.axis_size("dp")
    runs = pipe // count
    pairs = [
        (q * count + r, q * count + (r ^ bit))
        for q in range(pipe)
        for r in range(count)
        if (r ^ (q // runs)) % (2 * bit) == bit
    ]
    return lax.ppermute(blocks, BOTH, pairs)


def owner_to_first(blocks, run):
    pipe, count = lax.axis_size("pipe"), lax.axis_size("dp")
    runs = pipe // count
    return lax.ppermute(blocks, BOTH, [((runs * s + run) * count + s, s) for s in range(count)])


def exchanged(value, step):
    count = lax.axis_size("dp")
    return lax.ppermute(value, "dp", [(i, i ^ step) for i in range(count)])


def shards(section_inputs, arriving, top_grads, project_weights, output_weights):
    count = lax.axis_size("dp")
    pipe = lax.axis_size("pipe")
    me = lax.axis_index("dp")
    first = lax.axis_index("pipe") == 0
    _, ticks, seq, width = section_inputs.shape
    head = output_weights.shape[2]
    project, output = project_weights[0], output_weights[0]
    others, half = range(count), count // 2

    blocks, moved = top_grads, toward_owner(top_grads, 1)
    sent, scale = first_pieces(section_inputs[0], arriving[0], me, count)
    pieces = [shift(sent[j], j) for j in others]
    later_sent, later_scale = later_pieces(section_inputs[0], me, count)
    blocks = join_pieces(after(blocks, later_scale), moved)
    bit = 2
    while bit < count // 2:
        blocks = join_pieces(blocks, toward_owner(blocks, bit))
        bit *= 2
    moved = toward_owner(blocks, bit) if bit < count else None

    mine, other = first_partials(
        pieces, [scale, later_scale], after(project, blocks), output, me, width
    )
    below = lax.ppermute(
        after(output, other), "pipe", [(p, (p + 1) % pipe) for p in range(pipe)]
    )
    later_sent = after(tuple(later_sent), other)
    later = [shift(later_sent[j], j) for j in others]
    early = [later[j] for j in [2] if j < count]
    total = add_two(after(mine, below, *early), exchanged(other, 1))
    if moved is not None:
        blocks = join_pieces(after(blocks, total), moved)
    tops = [owner_to_first(blocks, run) for run in range(pipe // count)]
    later_mine, later_other = later_partials(later, after(project, total), me)
    step = 2
    while step < count:
        received = exchanged(total, step)
        total = add_two(after(total, later_other), received)
        step *= 2
    halves = [total, exchanged(total, 1)]
    later_total = add_two(later_mine, exchanged(later_other, 1))
    halves[0] = after(halves[0], later_total)
    later_parts, step = [later_total], 2
    while step < count:
        later_parts = [later_total, exchanged(later_total, step)]
        later_total = add_two(*later_parts)
        step *= 2

    first_grads = first_attention(halves, seq, half, head, ticks, width)
    passed, heads = middle_step(
        [after(first_grads[0], later_parts[-1]), first_grads[2]],
        pieces,
        tops,
        project,
        below,
        me,
        first,
    )
    later_halves = [later_total, exchanged(later_total, 1)]
    heads = [down(heads, j) for j in others[1:]]
    received = down(passed)
    later_grads = later_attention(
        later_halves, halves, heads, received, seq, half, head, ticks, me, width
    )
    back = last_step([later_grads[0], later_grads[2]], received, later, project, me)
    mixed = after(later_grads[1], back[0])
    back = [shift(back[j], -j) for j in others]
    project_grads, output_grads = weight_gradients(
        pieces, later, received, first_grads[:2], [later_grads[0], mixed], me
    )
    passed_back = join_features(back, me)
    return (project_grads[None], output_grads[None], passed_back[None])


def solution(mesh):
    in_specs = (
        P("pipe", None, "dp", None),
        P("pipe", "dp", None),
        P(None, "dp", "pipe"),
        P("pipe", "dp", None),
        P("pipe", "dp", None),
    )
    out_specs = (P("pipe", "dp", None), P("pipe", "dp", None), P("pipe", "dp", None))
    return jax.shard_map(shards, mesh=mesh, in_specs=in_specs, out_specs=out_specs, check_vma=False)
```

```python
import functools
import math

import jax
import jax.numpy as jnp
from jax import lax
from jax.experimental import pallas as pl
from jax.experimental.pallas import tpu as pltpu
from jax.sharding import PartitionSpec as P

EPSILON = 1e-06
CONTRACT_FIRST = (((0,), (0,)), ((), ()))
CONTRACT_LAST = (((1,), (1,)), ((), ()))
F32 = jnp.float32
BF16 = jnp.bfloat16
ROW_TILE = 16
LANES = 128
BOTH = ("pipe", "dp")


def shape(*dims, kind=BF16):
    return jax.ShapeDtypeStruct(dims, kind)


def kernel_call(body, outs, scalars, arrays, scratch=(), far=(), cost=1):
    return pl.pallas_call(
        body,
        out_shape=tuple(outs),
        in_specs=[pl.BlockSpec(memory_space=pltpu.SMEM)] * len(scalars)
        + [pl.BlockSpec(memory_space=pl.ANY)] * len(far)
        + [pl.BlockSpec(memory_space=pltpu.VMEM)] * len(arrays),
        out_specs=tuple(pl.BlockSpec(memory_space=pltpu.VMEM) for _ in outs),
        scratch_shapes=list(scratch),
        compiler_params=pltpu.CompilerParams(vmem_limit_bytes=24 * 1024 * 1024),
        cost_estimate=pl.CostEstimate(flops=1, bytes_accessed=cost, transcendentals=0),
    )(*[s.reshape(1).astype(jnp.int32) for s in scalars], *far, *arrays)


def dot(left, right, contract=(((1,), (0,)), ((), ()))):
    return lax.dot_general(left, right, contract, preferred_element_type=F32)


def normalize(values):
    centered = values - jnp.mean(values, axis=-1, keepdims=True)
    inverse = lax.rsqrt(jnp.mean(centered * centered, axis=-1, keepdims=True) + EPSILON)
    return (centered * inverse, inverse)


def norm_back(gradient, normed, inverse):
    centered = gradient - jnp.mean(gradient, axis=-1, keepdims=True)
    return inverse * (centered - normed * jnp.mean(gradient * normed, axis=-1, keepdims=True))


def column(row):
    return jnp.broadcast_to(row, (LANES, LANES)).T


def as_row(column):
    seq = column.shape[0]
    if seq < LANES:
        column = jnp.concatenate([column, jnp.zeros((LANES - seq, LANES), F32)], axis=0)
    return column.T[:1]


def split_two(value):
    high = value.astype(BF16).astype(F32)
    return high, value - high


def replica_of(me_ref, j, count):
    return lax.rem(me_ref[0] + count - j, count)


def block_rows(me_ref, j, count, seq):
    block = replica_of(me_ref, j, count) // 2 + (j % 2) * (count // 2)
    return pl.ds(pl.multiple_of(block * seq, seq), seq)


def first_pieces(inputs, arriving, me, count):
    seq, width = arriving.shape
    part = width // count

    def body(me_ref, x_ref, arriving_ref, *refs):
        outs, (scale_ref, hidden_ref) = refs[:count], refs[count:]
        for row in range(0, seq, ROW_TILE):
            rows = slice(row, row + ROW_TILE)
            normed, inverse = normalize(x_ref[0, rows, :].astype(F32))
            hidden_ref[rows, :] = normed.astype(BF16)
            scale_ref[rows, :] = jnp.broadcast_to(inverse, (ROW_TILE, LANES))
        for j in range(count):
            owner = lax.rem(me_ref[0] + j, count)
            columns = pl.ds(pl.multiple_of(owner * part, LANES), part)
            outs[j][0] = hidden_ref[:, columns]
            outs[j][1] = arriving_ref[:, columns]

    outs = [shape(2, seq, part)] * count + [shape(seq, LANES, kind=F32)]
    scratch = [pltpu.VMEM((seq, width), BF16)]
    result = kernel_call(body, outs, [me], [inputs, arriving], scratch)
    return list(result[:count]), result[count]


def later_pieces(inputs, me, count):
    _, seq, width = inputs.shape
    part = width // count

    def body(me_ref, x_ref, *refs):
        outs, (scale_ref, hidden_ref) = refs[:count], refs[count:]
        for row in range(0, seq, ROW_TILE):
            rows = slice(row, row + ROW_TILE)
            normed, inverse = normalize(x_ref[1, rows, :].astype(F32))
            hidden_ref[rows, :] = normed.astype(BF16)
            scale_ref[rows, :] = jnp.broadcast_to(inverse, (ROW_TILE, LANES))
        for j in range(count):
            owner = lax.rem(me_ref[0] + j, count)
            columns = pl.ds(pl.multiple_of(owner * part, LANES), part)
            outs[j][...] = hidden_ref[:, columns]

    outs = [shape(seq, part)] * count + [shape(seq, LANES, kind=F32)]
    scratch = [pltpu.VMEM((seq, width), BF16)]
    result = kernel_call(body, outs, [me], [inputs], scratch)
    return list(result[:count]), result[count]


def first_partials(pieces, scales, project, output, me, width):
    count = len(pieces)
    _, seq, part = pieces[0].shape
    wide, head = project.shape[1], output.shape[1]
    half, ticks = count // 2, len(scales)
    extra = -(-2 * ticks * half // ROW_TILE) * ROW_TILE

    def body(me_ref, *refs):
        piece_refs, refs = refs[:count], refs[count:]
        scale_refs, (project_ref, output_ref, *outs) = refs[:ticks], refs[ticks:]
        project = project_ref[...]
        for j in range(count):
            out_ref, rows = outs[j % 2], half_rows(me_ref, j, count, seq)
            out_ref[rows, :wide] = dot(piece_refs[j][0], project).astype(BF16)
            out_ref[rows, wide:] = dot(piece_refs[j][1], output_ref[...]).astype(BF16)
        sums = jnp.sum(project.astype(F32), axis=0, keepdims=True) / width
        place = lax.broadcasted_iota(jnp.int32, (extra, LANES), 0) - 2 * ticks * (me_ref[0] // 2)
        facts = jnp.zeros((extra, LANES), F32)
        for t in range(ticks):
            for index, value in enumerate(split_two(as_row(scale_refs[t][...]))):
                facts = jnp.where(place == 2 * t + index, value, facts)
        for out_ref, lanes in zip(outs, (facts, jnp.zeros((extra, LANES), F32))):
            out_ref[half * seq :, :LANES] = lanes.astype(BF16)
            out_ref[half * seq :, LANES:] = jnp.broadcast_to(sums, (extra, wide)).astype(BF16)

    outs = [shape(half * seq + extra, wide + head)] * 2
    return kernel_call(body, outs, [me], [*pieces, *scales, project, output])


def half_rows(me_ref, j, count, seq):
    block = replica_of(me_ref, j, count) // 2
    return pl.ds(pl.multiple_of(block * seq, seq), seq)


def later_partials(pieces, project, me):
    count = len(pieces)
    seq = pieces[0].shape[0]
    wide = project.shape[1]

    def body(me_ref, *refs):
        piece_refs, (project_ref, *outs) = refs[:count], refs[count:]
        for j in range(count):
            value = dot(piece_refs[j][...], project_ref[...])
            outs[j % 2][half_rows(me_ref, j, count, seq), :] = value.astype(BF16)

    return kernel_call(body, [shape(count // 2 * seq, wide)] * 2, [me], [*pieces, project])


def add_two(left, right):
    def body(left_ref, right_ref, out_ref):
        out_ref[...] = (left_ref[...].astype(F32) + right_ref[...].astype(F32)).astype(BF16)

    return kernel_call(body, [shape(*left.shape)], [], [left, right])[0]


def attention_back(projected, head_half, row_mean, scale, seq, outs, width):
    grad_ref, mixed_ref, numbers_ref = outs
    rows, head = head_half.shape
    count = rows // seq
    root = math.sqrt(head)
    query, query_scale = normalize(projected[:, :head])
    key, key_scale = normalize(projected[:, head : 2 * head])
    query_half, key_half = query.astype(BF16), key.astype(BF16)
    value_half = projected[:, 2 * head :].astype(BF16)

    def each(function, *values):
        return jnp.concatenate(
            [function(*(v[r * seq : (r + 1) * seq] for v in values)) for r in range(count)], axis=0
        )

    def last(left, right):
        return dot(left, right, CONTRACT_LAST)

    def leading(left, right):
        return dot(left, right, CONTRACT_FIRST)

    powered = jnp.exp(each(last, query_half, key_half) / root)
    attention = powered / jnp.sum(powered, axis=-1, keepdims=True)
    attention_half = attention.astype(BF16)
    mixed_ref[...] = each(dot, attention_half, value_half).astype(BF16)
    prob_grad = each(last, head_half, value_half)
    value_grad = each(leading, attention_half, head_half).astype(BF16)
    score_grad = (
        attention * (prob_grad - jnp.sum(attention * prob_grad, axis=-1, keepdims=True)) / root
    ).astype(BF16)
    query_grad = norm_back(each(dot, score_grad, key_half), query, query_scale)
    key_grad = norm_back(each(leading, score_grad, query_half), key, key_scale)
    proj_grad = jnp.concatenate(
        [query_grad.astype(BF16), key_grad.astype(BF16), value_grad], axis=1
    )
    grad_ref[...] = proj_grad
    spread = proj_grad.astype(F32)
    offset = scale * jnp.sum(spread * row_mean, axis=-1, keepdims=True)
    slope = scale * (jnp.sum(spread * projected, axis=-1, keepdims=True) / width)
    lane = lax.broadcasted_iota(jnp.int32, (rows, LANES), 1)
    numbers_ref[...] = jnp.where(lane == 0, scale, jnp.where(lane == 1, offset, slope))
    return proj_grad, offset, slope


def all_rows(half_refs, seq, half, columns):
    return jnp.concatenate([ref[: half * seq, columns] for ref in half_refs], axis=0).astype(F32)


def scale_column(half_refs, tick, ticks, seq, half):
    columns = []
    for ref in half_refs:
        facts = ref[half * seq :, :LANES].astype(F32)
        for block in range(half):
            row = 2 * (ticks * block + tick)
            columns.append(column(facts[row : row + 1] + facts[row + 1 : row + 2])[:seq, :1])
    return jnp.concatenate(columns, axis=0)


def attention_outs(rows, head):
    return [shape(rows, 3 * head), shape(rows, head), shape(rows, LANES, kind=F32)]


def below_parts(pieces, project, below, me):
    count, (_, seq, part) = len(pieces), pieces[0].shape
    wide, head = project.shape[1], below.shape[1]

    def body(me_ref, *refs):
        piece_refs, refs = refs[:count], refs[count:]
        project_ref, below_ref, rows_ref, product_ref, sums_ref = refs
        below = below_ref[...]
        for j in range(count):
            rows = block_rows(me_ref, j, count, seq)
            rows_ref[rows, :head] = dot(piece_refs[j][1], below)
            rows_ref[rows, head:] = dot(piece_refs[j][0], below)
        product_ref[...] = dot(project_ref[...], below, CONTRACT_FIRST).astype(BF16)
        sums = jnp.sum(below.astype(F32), axis=0, keepdims=True)
        sums_ref[...] = jnp.broadcast_to(sums, sums_ref.shape)

    outs = [
        shape(count * seq, 2 * head, kind=F32),
        shape(wide, head),
        shape(8, head, kind=F32),
    ]
    return kernel_call(body, outs, [me], [*pieces, project, below])


def first_attention(halves, parts, tops, below, seq, half, head, ticks, me, first, width):
    rows, wide, count, runs = 2 * half * seq, 3 * head, 2 * half, len(tops)
    run = below.shape[0] // runs

    def body(me_ref, first_ref, *refs):
        mine, (rows_ref, product_ref, sums_ref), refs = refs[:2], refs[2:5], refs[5:]
        top_refs, (below_ref, *outs, head_ref) = refs[:runs], refs[runs:]
        scale = scale_column(mine, 0, ticks, seq, half)
        proj_grad, offset, slope = attention_back(
            all_rows(mine, seq, half, slice(0, wide)),
            all_rows(mine, seq, half, slice(wide, wide + head)).astype(BF16),
            mine[0][half * seq :, LANES:].astype(F32)[:1],
            scale,
            seq,
            outs,
            width,
        )
        across = dot(proj_grad, product_ref[...])
        change = scale * across - offset * sums_ref[:1, :] - slope * rows_ref[:, head:]
        heads = (rows_ref[:, :head] + change).astype(BF16)
        for parity in range(2):
            for block in range(half):
                replica = 2 * block + lax.rem(me_ref[0] + parity, 2)
                start = (parity * half + block) * seq
                place = pl.ds(pl.multiple_of(replica * seq, seq), seq)
                head_ref[place, :] = heads[start : start + seq]

        @pl.when(first_ref[0] == 1)
        def _():
            for block in range(count):
                replica = lax.bitwise_xor(me_ref[0], block)
                place = pl.ds(pl.multiple_of(replica * seq, seq), seq)
                head_ref[place, :] = sum(
                    dot(top_refs[a][block], below_ref[a * run : (a + 1) * run, :])
                    for a in range(runs)
                ).astype(BF16)

    outs = [*attention_outs(rows, head), shape(rows, head)]
    arrays = [*halves, *parts, *tops, below]
    return kernel_call(body, outs, [me, first], arrays)


def sum_heads(heads, seq, me):
    rows, head = heads[0].shape
    half = rows // seq // 2

    def body(me_ref, *refs):
        for parity in range(2):
            for block in range(half):
                replica = 2 * block + lax.rem(me_ref[0] + parity, 2)
                place = pl.ds(pl.multiple_of(replica * seq, seq), seq)
                total = sum(ref[place, :].astype(F32) for ref in refs[:-1])
                start = (parity * half + block) * seq
                refs[-1][start : start + seq, :] = total.astype(BF16)

    return kernel_call(body, [shape(rows, head)], [me], heads, cost=1)[0]


def later_attention(halves, facts, head_half, seq, half, head, ticks, width):
    rows = 2 * half * seq

    def body(*refs):
        mine, facts, (head_ref, *outs) = refs[:2], refs[2:4], refs[4:]
        attention_back(
            all_rows(mine, seq, half, slice(None)),
            head_ref[...],
            facts[0][half * seq :, LANES:].astype(F32)[:1],
            scale_column(facts, 1, ticks, seq, half),
            seq,
            outs,
            width,
        )

    arrays = [*halves, *facts, head_half]
    return kernel_call(body, attention_outs(rows, head), [], arrays, cost=1)


def input_gradient(grad, numbers, incoming, hidden, project):
    scale, offset, slope = (numbers[:, i : i + 1] for i in range(3))
    hidden_grad = dot(grad, project, CONTRACT_LAST)
    change = scale * hidden_grad - offset - slope * hidden.astype(F32)
    return (incoming.astype(F32) + change).astype(BF16)


def middle_step(grads, pieces, tops, project, me, first):
    count, (_, seq, part) = len(pieces), pieces[0].shape
    runs = len(tops)
    run = part // runs

    def body(me_ref, first_ref, *refs):
        top_refs, piece_refs, refs = refs[:runs], refs[runs : runs + count], refs[runs + count :]
        grad_ref, numbers_ref, project_ref, passed_ref, sems = refs
        is_first = first_ref[0] == 1

        @pl.when(is_first)
        def _():
            copies = []
            for j in range(count):
                block = lax.bitwise_xor(me_ref[0], replica_of(me_ref, j, count))
                for a in range(runs):
                    place = passed_ref.at[j, :, pl.ds(a * run, run)]
                    copies.append(
                        pltpu.make_async_copy(top_refs[a].at[block], place, sems.at[j, a])
                    )
                    copies[-1].start()
            for copy in copies:
                copy.wait()

        @pl.when(jnp.logical_not(is_first))
        def _():
            for j in range(count):
                rows = block_rows(me_ref, j, count, seq)
                hidden, incoming = piece_refs[j][0], piece_refs[j][1]
                passed_ref[j] = input_gradient(
                    grad_ref[rows, :], numbers_ref[rows, :], incoming, hidden, project_ref[...]
                )

    scratch = [pltpu.SemaphoreType.DMA((count, runs))]
    arrays = [*pieces, *grads, project]
    outs = [shape(count, seq, part)]
    return kernel_call(body, outs, [me, first], arrays, scratch, far=tops)[0]


def last_step(grads, received, pieces, project, me):
    count, (seq, part) = len(pieces), pieces[0].shape

    def body(me_ref, *refs):
        piece_refs, (grad_ref, numbers_ref, received_ref, project_ref, *outs) = (
            refs[:count],
            refs[count:],
        )
        for j in range(count):
            rows = block_rows(me_ref, j, count, seq)
            outs[j][...] = input_gradient(
                grad_ref[rows, :],
                numbers_ref[rows, :],
                received_ref[j],
                piece_refs[j][...],
                project_ref[...],
            )

    arrays = [*pieces, *grads, received, project]
    return list(kernel_call(body, [shape(seq, part)] * count, [me], arrays))


def weight_gradients(pieces, later, received, first_grads, later_grads, me):
    count, (_, seq, part) = len(pieces), pieces[0].shape
    wide, head = first_grads[0].shape[1], first_grads[1].shape[1]
    block = min(part, 256)

    def body(me_ref, *refs):
        piece_refs, later_refs, refs = refs[:count], refs[count : 2 * count], refs[2 * count :]
        received_ref, grad0, mixed0, grad1, mixed1, project_ref, output_ref = refs
        for start in range(0, part, block):
            columns = slice(start, start + block)
            project_sum, output_sum = 0.0, 0.0
            for j in range(count):
                rows = block_rows(me_ref, j, count, seq)
                value = dot(piece_refs[j][0, :, columns], grad0[rows, :], CONTRACT_FIRST)
                value += dot(later_refs[j][:, columns], grad1[rows, :], CONTRACT_FIRST)
                project_sum += value.astype(BF16).astype(F32)
                value = dot(piece_refs[j][1, :, columns], mixed0[rows, :], CONTRACT_FIRST)
                value += dot(received_ref[j, :, columns], mixed1[rows, :], CONTRACT_FIRST)
                output_sum += value.astype(BF16).astype(F32)
            project_ref[columns, :] = project_sum
            output_ref[columns, :] = output_sum

    outs = [shape(part, wide, kind=F32), shape(part, head, kind=F32)]
    arrays = [*pieces, *later, received, *first_grads, *later_grads]
    return kernel_call(body, outs, [me], arrays)


def join_features(pieces, me):
    count = len(pieces)
    seq, part = pieces[0].shape

    def body(me_ref, *refs):
        for j in range(count):
            owner = lax.rem(me_ref[0] + j, count)
            columns = pl.ds(pl.multiple_of(owner * part, LANES), part)
            refs[count][:, columns] = refs[j][...]

    return kernel_call(body, [shape(seq, part * count)], [me], pieces)[0]


def shift(value, steps):
    count = lax.axis_size("dp")
    if steps % count == 0:
        return value
    return lax.ppermute(value, "dp", [(i, (i + steps) % count) for i in range(count)])


def after(value, *earlier):
    return lax.optimization_barrier((value, *earlier))[0]


def down(value, steps=0):
    pipe, count = lax.axis_size("pipe"), lax.axis_size("dp")
    pairs = [
        (p * count + r, (p - 1) % pipe * count + (r + steps) % count)
        for p in range(pipe)
        for r in range(count)
    ]
    return lax.ppermute(value, BOTH, pairs)


def join_pieces(left, right):
    size = left.shape[0]

    def body(left_ref, right_ref, out_ref):
        out_ref[:size] = left_ref[...]
        out_ref[size:] = right_ref[...]

    outs = [shape(2 * size, *left.shape[1:])]
    return kernel_call(body, outs, [], [left, right])[0]


def toward_owner(blocks, bit):
    pipe, count = lax.axis_size("pipe"), lax.axis_size("dp")
    runs = pipe // count
    pairs = [
        (q * count + r, q * count + (r ^ bit))
        for q in range(pipe)
        for r in range(count)
        if (r ^ (q // runs)) % (2 * bit) == bit
    ]
    return lax.ppermute(blocks, BOTH, pairs)


def owner_to_first(blocks, run):
    pipe, count = lax.axis_size("pipe"), lax.axis_size("dp")
    runs = pipe // count
    return lax.ppermute(blocks, BOTH, [((runs * s + run) * count + s, s) for s in range(count)])


def exchanged(value, step):
    count = lax.axis_size("dp")
    return lax.ppermute(value, "dp", [(i, i ^ step) for i in range(count)])


def shards(section_inputs, arriving, top_grads, project_weights, output_weights):
    count = lax.axis_size("dp")
    pipe = lax.axis_size("pipe")
    me = lax.axis_index("dp")
    first = lax.axis_index("pipe") == 0
    _, ticks, seq, width = section_inputs.shape
    head = output_weights.shape[2]
    project, output = project_weights[0], output_weights[0]
    others, half = range(count), count // 2

    blocks, moved = top_grads, toward_owner(top_grads, 1)
    sent, scale = first_pieces(section_inputs[0], arriving[0], me, count)
    pieces = [shift(sent[j], j) for j in others]
    later_sent, later_scale = later_pieces(section_inputs[0], me, count)
    blocks = join_pieces(after(blocks, later_scale), moved)
    bit = 2
    while bit < count // 2:
        blocks = join_pieces(blocks, toward_owner(blocks, bit))
        bit *= 2
    moved = toward_owner(blocks, bit) if bit < count else None

    mine, other = first_partials(
        pieces, [scale, later_scale], after(project, blocks), output, me, width
    )
    below = lax.ppermute(
        after(output, other), "pipe", [(p, (p + 1) % pipe) for p in range(pipe)]
    )
    later_sent = after(tuple(later_sent), other)
    later = [shift(later_sent[j], j) for j in others]
    early = [later[j] for j in [2] if j < count]
    total = add_two(after(mine, below, *early), exchanged(other, 1))
    if moved is not None:
        blocks = join_pieces(after(blocks, total), moved)
    tops = [owner_to_first(blocks, run) for run in range(pipe // count)]
    later_mine, later_other = later_partials(later, after(project, total), me)
    parts = below_parts(pieces, project, below, me)
    step = 2
    while step < count:
        received = exchanged(total, step)
        total = add_two(after(total, later_other), received)
        step *= 2
    halves = [total, exchanged(total, 1)]
    later_total = add_two(later_mine, exchanged(later_other, 1))
    halves[0] = after(halves[0], later_total)
    later_parts, step = [later_total], 2
    while step < count:
        later_parts = [later_total, exchanged(later_total, step)]
        later_total = add_two(*later_parts)
        step *= 2

    *first_grads, heads = first_attention(
        halves, parts, tops, below, seq, half, head, ticks, me, first, width
    )
    heads = [down(heads, j) for j in others]
    later_halves = [later_total, exchanged(later_total, 1)]
    passed = middle_step([first_grads[0], first_grads[2]], pieces, tops, project, me, first)
    received = down(after(passed, later_parts[-1]))
    head_half = sum_heads(heads, seq, me)
    later_grads = later_attention(
        later_halves, halves, head_half, seq, half, head, ticks, width
    )
    back = last_step([later_grads[0], later_grads[2]], received, later, project, me)
    mixed = after(later_grads[1], back[0])
    back = [shift(back[j], -j) for j in others]
    project_grads, output_grads = weight_gradients(
        pieces, later, received, first_grads[:2], [later_grads[0], mixed], me
    )
    passed_back = join_features(back, me)
    return (project_grads[None], output_grads[None], passed_back[None])


def solution(mesh):
    in_specs = (
        P("pipe", None, "dp", None),
        P("pipe", "dp", None),
        P(None, "dp", "pipe"),
        P("pipe", "dp", None),
        P("pipe", "dp", None),
    )
    out_specs = (P("pipe", "dp", None), P("pipe", "dp", None), P("pipe", "dp", None))
    return jax.shard_map(shards, mesh=mesh, in_specs=in_specs, out_specs=out_specs, check_vma=False)
```

```python
import functools
import math

import jax
import jax.numpy as jnp
from jax import lax
from jax.experimental import pallas as pl
from jax.experimental.pallas import tpu as pltpu
from jax.sharding import PartitionSpec as P

EPSILON = 1e-06
CONTRACT_FIRST = (((0,), (0,)), ((), ()))
CONTRACT_LAST = (((1,), (1,)), ((), ()))
F32 = jnp.float32
BF16 = jnp.bfloat16
ROW_TILE = 16
LANES = 128
BOTH = ("pipe", "dp")


def shape(*dims, kind=BF16):
    return jax.ShapeDtypeStruct(dims, kind)


def kernel_call(body, outs, scalars, arrays, scratch=(), far=(), cost=1):
    return pl.pallas_call(
        body,
        out_shape=tuple(outs),
        in_specs=[pl.BlockSpec(memory_space=pltpu.SMEM)] * len(scalars)
        + [pl.BlockSpec(memory_space=pl.ANY)] * len(far)
        + [pl.BlockSpec(memory_space=pltpu.VMEM)] * len(arrays),
        out_specs=tuple(pl.BlockSpec(memory_space=pltpu.VMEM) for _ in outs),
        scratch_shapes=list(scratch),
        compiler_params=pltpu.CompilerParams(vmem_limit_bytes=24 * 1024 * 1024),
        cost_estimate=pl.CostEstimate(flops=1, bytes_accessed=cost, transcendentals=0),
    )(*[s.reshape(1).astype(jnp.int32) for s in scalars], *far, *arrays)


def dot(left, right, contract=(((1,), (0,)), ((), ()))):
    return lax.dot_general(left, right, contract, preferred_element_type=F32)


def normalize(values):
    centered = values - jnp.mean(values, axis=-1, keepdims=True)
    inverse = lax.rsqrt(jnp.mean(centered * centered, axis=-1, keepdims=True) + EPSILON)
    return (centered * inverse, inverse)


def norm_back(gradient, normed, inverse):
    centered = gradient - jnp.mean(gradient, axis=-1, keepdims=True)
    return inverse * (centered - normed * jnp.mean(gradient * normed, axis=-1, keepdims=True))


def column(row):
    return jnp.broadcast_to(row, (LANES, LANES)).T


def as_row(column):
    seq = column.shape[0]
    if seq < LANES:
        column = jnp.concatenate([column, jnp.zeros((LANES - seq, LANES), F32)], axis=0)
    return column.T[:1]


def split_two(value):
    high = value.astype(BF16).astype(F32)
    return high, value - high


def replica_of(me_ref, j, count):
    return lax.rem(me_ref[0] + count - j, count)


def block_rows(me_ref, j, count, seq):
    block = replica_of(me_ref, j, count) // 2 + (j % 2) * (count // 2)
    return pl.ds(pl.multiple_of(block * seq, seq), seq)


def first_pieces(inputs, arriving, me, count):
    seq, width = arriving.shape
    part = width // count

    def body(me_ref, x_ref, arriving_ref, *refs):
        outs, (scale_ref, hidden_ref) = refs[:count], refs[count:]
        for row in range(0, seq, ROW_TILE):
            rows = slice(row, row + ROW_TILE)
            normed, inverse = normalize(x_ref[0, rows, :].astype(F32))
            hidden_ref[rows, :] = normed.astype(BF16)
            scale_ref[rows, :] = jnp.broadcast_to(inverse, (ROW_TILE, LANES))
        for j in range(count):
            owner = lax.rem(me_ref[0] + j, count)
            columns = pl.ds(pl.multiple_of(owner * part, LANES), part)
            outs[j][0] = hidden_ref[:, columns]
            outs[j][1] = arriving_ref[:, columns]

    outs = [shape(2, seq, part)] * count + [shape(seq, LANES, kind=F32)]
    scratch = [pltpu.VMEM((seq, width), BF16)]
    result = kernel_call(body, outs, [me], [inputs, arriving], scratch)
    return list(result[:count]), result[count]


def later_pieces(inputs, me, count):
    _, seq, width = inputs.shape
    part = width // count

    def body(me_ref, x_ref, *refs):
        outs, (scale_ref, hidden_ref) = refs[:count], refs[count:]
        for row in range(0, seq, ROW_TILE):
            rows = slice(row, row + ROW_TILE)
            normed, inverse = normalize(x_ref[1, rows, :].astype(F32))
            hidden_ref[rows, :] = normed.astype(BF16)
            scale_ref[rows, :] = jnp.broadcast_to(inverse, (ROW_TILE, LANES))
        for j in range(count):
            owner = lax.rem(me_ref[0] + j, count)
            columns = pl.ds(pl.multiple_of(owner * part, LANES), part)
            outs[j][...] = hidden_ref[:, columns]

    outs = [shape(seq, part)] * count + [shape(seq, LANES, kind=F32)]
    scratch = [pltpu.VMEM((seq, width), BF16)]
    result = kernel_call(body, outs, [me], [inputs], scratch)
    return list(result[:count]), result[count]


def first_partials(pieces, scales, project, output, me, width):
    count = len(pieces)
    _, seq, part = pieces[0].shape
    wide, head = project.shape[1], output.shape[1]
    half, ticks = count // 2, len(scales)
    extra = -(-2 * ticks * half // ROW_TILE) * ROW_TILE

    def body(me_ref, *refs):
        piece_refs, refs = refs[:count], refs[count:]
        scale_refs, (project_ref, output_ref, *outs) = refs[:ticks], refs[ticks:]
        project = project_ref[...]
        hidden = jnp.concatenate([ref[0] for ref in piece_refs], axis=0)
        projected = dot(hidden, project).astype(BF16)
        incoming = jnp.concatenate([ref[1] for ref in piece_refs], axis=0)
        heads = dot(incoming, output_ref[...]).astype(BF16)
        for j in range(count):
            out_ref, rows = outs[j % 2], half_rows(me_ref, j, count, seq)
            place = slice(j * seq, (j + 1) * seq)
            out_ref[rows, :wide] = projected[place]
            out_ref[rows, wide:] = heads[place]
        sums = jnp.sum(project.astype(F32), axis=0, keepdims=True) / width
        place = lax.broadcasted_iota(jnp.int32, (extra, LANES), 0) - 2 * ticks * (me_ref[0] // 2)
        facts = jnp.zeros((extra, LANES), F32)
        for t in range(ticks):
            for index, value in enumerate(split_two(as_row(scale_refs[t][...]))):
                facts = jnp.where(place == 2 * t + index, value, facts)
        for out_ref, lanes in zip(outs, (facts, jnp.zeros((extra, LANES), F32))):
            out_ref[half * seq :, :LANES] = lanes.astype(BF16)
            out_ref[half * seq :, LANES:] = jnp.broadcast_to(sums, (extra, wide)).astype(BF16)

    outs = [shape(half * seq + extra, wide + head)] * 2
    return kernel_call(body, outs, [me], [*pieces, *scales, project, output])


def half_rows(me_ref, j, count, seq):
    block = replica_of(me_ref, j, count) // 2
    return pl.ds(pl.multiple_of(block * seq, seq), seq)


def later_partials(pieces, project, me):
    count = len(pieces)
    seq = pieces[0].shape[0]
    wide = project.shape[1]

    def body(me_ref, *refs):
        piece_refs, (project_ref, *outs) = refs[:count], refs[count:]
        hidden = jnp.concatenate([ref[...] for ref in piece_refs], axis=0)
        value = dot(hidden, project_ref[...]).astype(BF16)
        for j in range(count):
            rows = half_rows(me_ref, j, count, seq)
            outs[j % 2][rows, :] = value[j * seq : (j + 1) * seq]

    return kernel_call(body, [shape(count // 2 * seq, wide)] * 2, [me], [*pieces, project])


def add_two(left, right):
    def body(left_ref, right_ref, out_ref):
        out_ref[...] = (left_ref[...].astype(F32) + right_ref[...].astype(F32)).astype(BF16)

    return kernel_call(body, [shape(*left.shape)], [], [left, right])[0]


def attention_back(projected, head_half, row_mean, scale, seq, outs, width):
    grad_ref, mixed_ref, numbers_ref = outs
    rows, head = head_half.shape
    count = rows // seq
    root = math.sqrt(head)
    query, query_scale = normalize(projected[:, :head])
    key, key_scale = normalize(projected[:, head : 2 * head])
    query_half, key_half = query.astype(BF16), key.astype(BF16)
    value_half = projected[:, 2 * head :].astype(BF16)

    def each(function, *values):
        return jnp.concatenate(
            [function(*(v[r * seq : (r + 1) * seq] for v in values)) for r in range(count)], axis=0
        )

    def last(left, right):
        return dot(left, right, CONTRACT_LAST)

    def leading(left, right):
        return dot(left, right, CONTRACT_FIRST)

    powered = jnp.exp(each(last, query_half, key_half) / root)
    attention = powered / jnp.sum(powered, axis=-1, keepdims=True)
    attention_half = attention.astype(BF16)
    mixed_ref[...] = each(dot, attention_half, value_half).astype(BF16)
    prob_grad = each(last, head_half, value_half)
    value_grad = each(leading, attention_half, head_half).astype(BF16)
    score_grad = (
        attention * (prob_grad - jnp.sum(attention * prob_grad, axis=-1, keepdims=True)) / root
    ).astype(BF16)
    query_grad = norm_back(each(dot, score_grad, key_half), query, query_scale)
    key_grad = norm_back(each(leading, score_grad, query_half), key, key_scale)
    proj_grad = jnp.concatenate(
        [query_grad.astype(BF16), key_grad.astype(BF16), value_grad], axis=1
    )
    grad_ref[...] = proj_grad
    spread = proj_grad.astype(F32)
    offset = scale * jnp.sum(spread * row_mean, axis=-1, keepdims=True)
    slope = scale * (jnp.sum(spread * projected, axis=-1, keepdims=True) / width)
    lane = lax.broadcasted_iota(jnp.int32, (rows, LANES), 1)
    numbers_ref[...] = jnp.where(lane == 0, scale, jnp.where(lane == 1, offset, slope))
    return proj_grad, offset, slope


def all_rows(half_refs, seq, half, columns):
    return jnp.concatenate([ref[: half * seq, columns] for ref in half_refs], axis=0).astype(F32)


def scale_column(half_refs, tick, ticks, seq, half):
    columns = []
    for ref in half_refs:
        facts = ref[half * seq :, :LANES].astype(F32)
        for block in range(half):
            row = 2 * (ticks * block + tick)
            columns.append(column(facts[row : row + 1] + facts[row + 1 : row + 2])[:seq, :1])
    return jnp.concatenate(columns, axis=0)


def attention_outs(rows, head):
    return [shape(rows, 3 * head), shape(rows, head), shape(rows, LANES, kind=F32)]


def below_parts(pieces, project, below, me):
    count, (_, seq, part) = len(pieces), pieces[0].shape
    wide, head = project.shape[1], below.shape[1]

    def body(me_ref, *refs):
        piece_refs, refs = refs[:count], refs[count:]
        project_ref, below_ref, rows_ref, product_ref, sums_ref = refs
        below = below_ref[...]
        for j in range(count):
            rows = block_rows(me_ref, j, count, seq)
            rows_ref[rows, :head] = dot(piece_refs[j][1], below)
            rows_ref[rows, head:] = dot(piece_refs[j][0], below)
        product_ref[...] = dot(project_ref[...], below, CONTRACT_FIRST).astype(BF16)
        sums = jnp.sum(below.astype(F32), axis=0, keepdims=True)
        sums_ref[...] = jnp.broadcast_to(sums, sums_ref.shape)

    outs = [
        shape(count * seq, 2 * head, kind=F32),
        shape(wide, head),
        shape(8, head, kind=F32),
    ]
    return kernel_call(body, outs, [me], [*pieces, project, below])


def first_attention(halves, parts, tops, below, seq, half, head, ticks, me, first, width):
    rows, wide, count, runs = 2 * half * seq, 3 * head, 2 * half, len(tops)
    run = below.shape[0] // runs

    def body(me_ref, first_ref, *refs):
        mine, (rows_ref, product_ref, sums_ref), refs = refs[:2], refs[2:5], refs[5:]
        top_refs, (below_ref, *outs, head_ref) = refs[:runs], refs[runs:]
        scale = scale_column(mine, 0, ticks, seq, half)
        proj_grad, offset, slope = attention_back(
            all_rows(mine, seq, half, slice(0, wide)),
            all_rows(mine, seq, half, slice(wide, wide + head)).astype(BF16),
            mine[0][half * seq :, LANES:].astype(F32)[:1],
            scale,
            seq,
            outs,
            width,
        )
        across = dot(proj_grad, product_ref[...])
        change = scale * across - offset * sums_ref[:1, :] - slope * rows_ref[:, head:]
        heads = (rows_ref[:, :head] + change).astype(BF16)
        for parity in range(2):
            for block in range(half):
                replica = 2 * block + lax.rem(me_ref[0] + parity, 2)
                start = (parity * half + block) * seq
                place = pl.ds(pl.multiple_of(replica * seq, seq), seq)
                head_ref[place, :] = heads[start : start + seq]

        @pl.when(first_ref[0] == 1)
        def _():
            for block in range(count):
                replica = lax.bitwise_xor(me_ref[0], block)
                place = pl.ds(pl.multiple_of(replica * seq, seq), seq)
                head_ref[place, :] = sum(
                    dot(top_refs[a][block], below_ref[a * run : (a + 1) * run, :])
                    for a in range(runs)
                ).astype(BF16)

    outs = [*attention_outs(rows, head), shape(rows, head)]
    arrays = [*halves, *parts, *tops, below]
    return kernel_call(body, outs, [me, first], arrays)


def sum_heads(heads, seq, me):
    rows, head = heads[0].shape
    half = rows // seq // 2

    def body(me_ref, *refs):
        for parity in range(2):
            for block in range(half):
                replica = 2 * block + lax.rem(me_ref[0] + parity, 2)
                place = pl.ds(pl.multiple_of(replica * seq, seq), seq)
                total = sum(ref[place, :].astype(F32) for ref in refs[:-1])
                start = (parity * half + block) * seq
                refs[-1][start : start + seq, :] = total.astype(BF16)

    return kernel_call(body, [shape(rows, head)], [me], heads, cost=1)[0]


def later_attention(halves, facts, head_half, seq, half, head, ticks, width):
    rows = 2 * half * seq

    def body(*refs):
        mine, facts, (head_ref, *outs) = refs[:2], refs[2:4], refs[4:]
        attention_back(
            all_rows(mine, seq, half, slice(None)),
            head_ref[...],
            facts[0][half * seq :, LANES:].astype(F32)[:1],
            scale_column(facts, 1, ticks, seq, half),
            seq,
            outs,
            width,
        )

    arrays = [*halves, *facts, head_half]
    return kernel_call(body, attention_outs(rows, head), [], arrays, cost=1)


def input_gradient(hidden_grad, numbers, incoming, hidden):
    scale, offset, slope = (numbers[:, i : i + 1] for i in range(3))
    change = scale * hidden_grad - offset - slope * hidden.astype(F32)
    return (incoming.astype(F32) + change).astype(BF16)


def middle_step(grads, pieces, tops, project, me, first):
    count, (_, seq, part) = len(pieces), pieces[0].shape
    runs = len(tops)
    run = part // runs

    def body(me_ref, first_ref, *refs):
        top_refs, piece_refs, refs = refs[:runs], refs[runs : runs + count], refs[runs + count :]
        grad_ref, numbers_ref, project_ref, passed_ref, sems, wide_ref = refs
        is_first = first_ref[0] == 1

        @pl.when(is_first)
        def _():
            copies = []
            for j in range(count):
                block = lax.bitwise_xor(me_ref[0], replica_of(me_ref, j, count))
                for a in range(runs):
                    place = passed_ref.at[j, :, pl.ds(a * run, run)]
                    copies.append(
                        pltpu.make_async_copy(top_refs[a].at[block], place, sems.at[j, a])
                    )
                    copies[-1].start()
            for copy in copies:
                copy.wait()

        @pl.when(jnp.logical_not(is_first))
        def _():
            wide_ref[...] = dot(grad_ref[...], project_ref[...], CONTRACT_LAST)
            for j in range(count):
                rows = block_rows(me_ref, j, count, seq)
                hidden, incoming = piece_refs[j][0], piece_refs[j][1]
                passed_ref[j] = input_gradient(
                    wide_ref[rows, :], numbers_ref[rows, :], incoming, hidden
                )

    scratch = [
        pltpu.SemaphoreType.DMA((count, runs)),
        pltpu.VMEM((count * seq, part), F32),
    ]
    arrays = [*pieces, *grads, project]
    outs = [shape(count, seq, part)]
    return kernel_call(body, outs, [me, first], arrays, scratch, far=tops)[0]


def last_step(grads, received, pieces, project, me):
    count, (seq, part) = len(pieces), pieces[0].shape

    def body(me_ref, *refs):
        piece_refs, refs = refs[:count], refs[count:]
        grad_ref, numbers_ref, received_ref, project_ref, *outs, wide_ref = refs
        wide_ref[...] = dot(grad_ref[...], project_ref[...], CONTRACT_LAST)
        for j in range(count):
            rows = block_rows(me_ref, j, count, seq)
            outs[j][...] = input_gradient(
                wide_ref[rows, :], numbers_ref[rows, :], received_ref[j], piece_refs[j][...]
            )

    arrays = [*pieces, *grads, received, project]
    scratch = [pltpu.VMEM((count * seq, part), F32)]
    return list(kernel_call(body, [shape(seq, part)] * count, [me], arrays, scratch))


def weight_gradients(pieces, later, received, first_grads, later_grads, me):
    count, (_, seq, part) = len(pieces), pieces[0].shape
    wide, head = first_grads[0].shape[1], first_grads[1].shape[1]
    block = min(part, 256)

    def body(me_ref, *refs):
        piece_refs, later_refs, refs = refs[:count], refs[count : 2 * count], refs[2 * count :]
        received_ref, grad0, mixed0, grad1, mixed1, project_ref, output_ref = refs
        for start in range(0, part, block):
            columns = slice(start, start + block)
            project_sum, output_sum = 0.0, 0.0
            for j in range(count):
                rows = block_rows(me_ref, j, count, seq)
                value = dot(piece_refs[j][0, :, columns], grad0[rows, :], CONTRACT_FIRST)
                value += dot(later_refs[j][:, columns], grad1[rows, :], CONTRACT_FIRST)
                project_sum += value.astype(BF16).astype(F32)
                value = dot(piece_refs[j][1, :, columns], mixed0[rows, :], CONTRACT_FIRST)
                value += dot(received_ref[j, :, columns], mixed1[rows, :], CONTRACT_FIRST)
                output_sum += value.astype(BF16).astype(F32)
            project_ref[columns, :] = project_sum
            output_ref[columns, :] = output_sum

    outs = [shape(part, wide, kind=F32), shape(part, head, kind=F32)]
    arrays = [*pieces, *later, received, *first_grads, *later_grads]
    return kernel_call(body, outs, [me], arrays)


def join_features(pieces, me):
    count = len(pieces)
    seq, part = pieces[0].shape

    def body(me_ref, *refs):
        for j in range(count):
            owner = lax.rem(me_ref[0] + j, count)
            columns = pl.ds(pl.multiple_of(owner * part, LANES), part)
            refs[count][:, columns] = refs[j][...]

    return kernel_call(body, [shape(seq, part * count)], [me], pieces)[0]


def shift(value, steps):
    count = lax.axis_size("dp")
    if steps % count == 0:
        return value
    return lax.ppermute(value, "dp", [(i, (i + steps) % count) for i in range(count)])


def after(value, *earlier):
    return lax.optimization_barrier((value, *earlier))[0]


def down(value, steps=0):
    pipe, count = lax.axis_size("pipe"), lax.axis_size("dp")
    pairs = [
        (p * count + r, (p - 1) % pipe * count + (r + steps) % count)
        for p in range(pipe)
        for r in range(count)
    ]
    return lax.ppermute(value, BOTH, pairs)


def join_pieces(left, right):
    size = left.shape[0]

    def body(left_ref, right_ref, out_ref):
        out_ref[:size] = left_ref[...]
        out_ref[size:] = right_ref[...]

    outs = [shape(2 * size, *left.shape[1:])]
    return kernel_call(body, outs, [], [left, right])[0]


def toward_owner(blocks, bit):
    pipe, count = lax.axis_size("pipe"), lax.axis_size("dp")
    runs = pipe // count
    pairs = [
        (q * count + r, q * count + (r ^ bit))
        for q in range(pipe)
        for r in range(count)
        if (r ^ (q // runs)) % (2 * bit) == bit
    ]
    return lax.ppermute(blocks, BOTH, pairs)


def owner_to_first(blocks, run):
    pipe, count = lax.axis_size("pipe"), lax.axis_size("dp")
    runs = pipe // count
    return lax.ppermute(blocks, BOTH, [((runs * s + run) * count + s, s) for s in range(count)])


def exchanged(value, step):
    count = lax.axis_size("dp")
    return lax.ppermute(value, "dp", [(i, i ^ step) for i in range(count)])


def shards(section_inputs, arriving, top_grads, project_weights, output_weights):
    count = lax.axis_size("dp")
    pipe = lax.axis_size("pipe")
    me = lax.axis_index("dp")
    first = lax.axis_index("pipe") == 0
    _, ticks, seq, width = section_inputs.shape
    head = output_weights.shape[2]
    project, output = project_weights[0], output_weights[0]
    others, half = range(count), count // 2

    blocks, moved = top_grads, toward_owner(top_grads, 1)
    sent, scale = first_pieces(section_inputs[0], arriving[0], me, count)
    pieces = [shift(sent[j], j) for j in others]
    later_sent, later_scale = later_pieces(section_inputs[0], me, count)
    blocks = join_pieces(after(blocks, later_scale), moved)
    bit = 2
    while bit < count // 2:
        blocks = join_pieces(blocks, toward_owner(blocks, bit))
        bit *= 2
    moved = toward_owner(blocks, bit) if bit < count else None

    mine, other = first_partials(
        pieces, [scale, later_scale], after(project, blocks), output, me, width
    )
    below = lax.ppermute(
        after(output, other), "pipe", [(p, (p + 1) % pipe) for p in range(pipe)]
    )
    later_sent = after(tuple(later_sent), other)
    later = [shift(later_sent[j], j) for j in others]
    early = [later[j] for j in [2] if j < count]
    total = add_two(after(mine, below, *early), exchanged(other, 1))
    if moved is not None:
        blocks = join_pieces(after(blocks, total), moved)
    tops = [owner_to_first(blocks, run) for run in range(pipe // count)]
    later_mine, later_other = later_partials(later, after(project, total), me)
    parts = below_parts(pieces, project, below, me)
    step = 2
    while step < count:
        received = exchanged(total, step)
        total = add_two(after(total, later_other), received)
        step *= 2
    halves = [total, exchanged(total, 1)]
    later_total = add_two(later_mine, exchanged(later_other, 1))
    halves[0] = after(halves[0], later_total)
    later_parts, step = [later_total], 2
    while step < count:
        later_parts = [later_total, exchanged(later_total, step)]
        later_total = add_two(*later_parts)
        step *= 2

    *first_grads, heads = first_attention(
        halves, parts, tops, below, seq, half, head, ticks, me, first, width
    )
    heads = [down(heads, j) for j in others]
    later_halves = [later_total, exchanged(later_total, 1)]
    passed = middle_step([first_grads[0], first_grads[2]], pieces, tops, project, me, first)
    received = down(after(passed, later_parts[-1]))
    head_half = sum_heads(heads, seq, me)
    later_grads = later_attention(
        later_halves, halves, head_half, seq, half, head, ticks, width
    )
    back = last_step([later_grads[0], later_grads[2]], received, later, project, me)
    mixed = after(later_grads[1], back[0])
    back = [shift(back[j], -j) for j in others]
    project_grads, output_grads = weight_gradients(
        pieces, later, received, first_grads[:2], [later_grads[0], mixed], me
    )
    passed_back = join_features(back, me)
    return (project_grads[None], output_grads[None], passed_back[None])


def solution(mesh):
    in_specs = (
        P("pipe", None, "dp", None),
        P("pipe", "dp", None),
        P(None, "dp", "pipe"),
        P("pipe", "dp", None),
        P("pipe", "dp", None),
    )
    out_specs = (P("pipe", "dp", None), P("pipe", "dp", None), P("pipe", "dp", None))
    return jax.shard_map(shards, mesh=mesh, in_specs=in_specs, out_specs=out_specs, check_vma=False)
```

```python
import functools
import math

import jax
import jax.numpy as jnp
from jax import lax
from jax.experimental import pallas as pl
from jax.experimental.pallas import tpu as pltpu
from jax.sharding import PartitionSpec as P

EPSILON = 1e-06
CONTRACT_FIRST = (((0,), (0,)), ((), ()))
CONTRACT_LAST = (((1,), (1,)), ((), ()))
F32 = jnp.float32
BF16 = jnp.bfloat16
ROW_TILE = 16
LANES = 128
BOTH = ("pipe", "dp")


def shape(*dims, kind=BF16):
    return jax.ShapeDtypeStruct(dims, kind)


def kernel_call(body, outs, scalars, arrays, scratch=(), far=(), cost=1):
    return pl.pallas_call(
        body,
        out_shape=tuple(outs),
        in_specs=[pl.BlockSpec(memory_space=pltpu.SMEM)] * len(scalars)
        + [pl.BlockSpec(memory_space=pl.ANY)] * len(far)
        + [pl.BlockSpec(memory_space=pltpu.VMEM)] * len(arrays),
        out_specs=tuple(pl.BlockSpec(memory_space=pltpu.VMEM) for _ in outs),
        scratch_shapes=list(scratch),
        compiler_params=pltpu.CompilerParams(vmem_limit_bytes=24 * 1024 * 1024),
        cost_estimate=pl.CostEstimate(flops=1, bytes_accessed=cost, transcendentals=0),
    )(*[s.reshape(1).astype(jnp.int32) for s in scalars], *far, *arrays)


def dot(left, right, contract=(((1,), (0,)), ((), ()))):
    return lax.dot_general(left, right, contract, preferred_element_type=F32)


def normalize(values):
    centered = values - jnp.mean(values, axis=-1, keepdims=True)
    inverse = lax.rsqrt(jnp.mean(centered * centered, axis=-1, keepdims=True) + EPSILON)
    return (centered * inverse, inverse)


def norm_back(gradient, normed, inverse):
    centered = gradient - jnp.mean(gradient, axis=-1, keepdims=True)
    return inverse * (centered - normed * jnp.mean(gradient * normed, axis=-1, keepdims=True))


def column(row):
    return jnp.broadcast_to(row, (LANES, LANES)).T


def as_row(column):
    seq = column.shape[0]
    if seq < LANES:
        column = jnp.concatenate([column, jnp.zeros((LANES - seq, LANES), F32)], axis=0)
    return column.T[:1]


def split_two(value):
    high = value.astype(BF16).astype(F32)
    return high, value - high


def replica_of(me_ref, j, count):
    return lax.rem(me_ref[0] + count - j, count)


def block_rows(me_ref, j, count, seq):
    block = replica_of(me_ref, j, count) // 2 + (j % 2) * (count // 2)
    return pl.ds(pl.multiple_of(block * seq, seq), seq)


def first_pieces(inputs, arriving, me, count):
    seq, width = arriving.shape
    part = width // count

    def body(me_ref, x_ref, arriving_ref, *refs):
        outs, (scale_ref, hidden_ref) = refs[:count], refs[count:]
        for row in range(0, seq, ROW_TILE):
            rows = slice(row, row + ROW_TILE)
            normed, inverse = normalize(x_ref[0, rows, :].astype(F32))
            hidden_ref[rows, :] = normed.astype(BF16)
            scale_ref[rows, :] = jnp.broadcast_to(inverse, (ROW_TILE, LANES))
        for j in range(count):
            owner = lax.rem(me_ref[0] + j, count)
            columns = pl.ds(pl.multiple_of(owner * part, LANES), part)
            outs[j][0] = hidden_ref[:, columns]
            outs[j][1] = arriving_ref[:, columns]

    outs = [shape(2, seq, part)] * count + [shape(seq, LANES, kind=F32)]
    scratch = [pltpu.VMEM((seq, width), BF16)]
    result = kernel_call(body, outs, [me], [inputs, arriving], scratch)
    return list(result[:count]), result[count]


def later_pieces(inputs, me, count):
    _, seq, width = inputs.shape
    part = width // count

    def body(me_ref, x_ref, *refs):
        outs, (scale_ref, hidden_ref) = refs[:count], refs[count:]
        for row in range(0, seq, ROW_TILE):
            rows = slice(row, row + ROW_TILE)
            normed, inverse = normalize(x_ref[1, rows, :].astype(F32))
            hidden_ref[rows, :] = normed.astype(BF16)
            scale_ref[rows, :] = jnp.broadcast_to(inverse, (ROW_TILE, LANES))
        for j in range(count):
            owner = lax.rem(me_ref[0] + j, count)
            columns = pl.ds(pl.multiple_of(owner * part, LANES), part)
            outs[j][...] = hidden_ref[:, columns]

    outs = [shape(seq, part)] * count + [shape(seq, LANES, kind=F32)]
    scratch = [pltpu.VMEM((seq, width), BF16)]
    result = kernel_call(body, outs, [me], [inputs], scratch)
    return list(result[:count]), result[count]


def first_partials(pieces, scales, project, output, me, width):
    count = len(pieces)
    _, seq, part = pieces[0].shape
    wide, head = project.shape[1], output.shape[1]
    half, ticks = count // 2, len(scales)
    extra = -(-2 * ticks * half // ROW_TILE) * ROW_TILE

    def body(me_ref, *refs):
        piece_refs, refs = refs[:count], refs[count:]
        scale_refs, (project_ref, output_ref, *outs) = refs[:ticks], refs[ticks:]
        project = project_ref[...]
        hidden = jnp.concatenate([ref[0] for ref in piece_refs], axis=0)
        projected = dot(hidden, project).astype(BF16)
        incoming = jnp.concatenate([ref[1] for ref in piece_refs], axis=0)
        heads = dot(incoming, output_ref[...]).astype(BF16)
        for j in range(count):
            out_ref, rows = outs[j % 2], half_rows(me_ref, j, count, seq)
            place = slice(j * seq, (j + 1) * seq)
            out_ref[rows, :wide] = projected[place]
            out_ref[rows, wide:] = heads[place]
        sums = jnp.sum(project.astype(F32), axis=0, keepdims=True) / width
        place = lax.broadcasted_iota(jnp.int32, (extra, LANES), 0) - 2 * ticks * (me_ref[0] // 2)
        facts = jnp.zeros((extra, LANES), F32)
        for t in range(ticks):
            for index, value in enumerate(split_two(as_row(scale_refs[t][...]))):
                facts = jnp.where(place == 2 * t + index, value, facts)
        for out_ref, lanes in zip(outs, (facts, jnp.zeros((extra, LANES), F32))):
            out_ref[half * seq :, :LANES] = lanes.astype(BF16)
            out_ref[half * seq :, LANES:] = two_terms(sums, extra)

    outs = [shape(half * seq + extra, wide + head)] * 2
    return kernel_call(body, outs, [me], [*pieces, *scales, project, output])


def half_rows(me_ref, j, count, seq):
    block = replica_of(me_ref, j, count) // 2
    return pl.ds(pl.multiple_of(block * seq, seq), seq)


def later_partials(pieces, project, me):
    count = len(pieces)
    seq = pieces[0].shape[0]
    wide = project.shape[1]

    def body(me_ref, *refs):
        piece_refs, (project_ref, *outs) = refs[:count], refs[count:]
        hidden = jnp.concatenate([ref[...] for ref in piece_refs], axis=0)
        value = dot(hidden, project_ref[...]).astype(BF16)
        for j in range(count):
            rows = half_rows(me_ref, j, count, seq)
            outs[j % 2][rows, :] = value[j * seq : (j + 1) * seq]

    return kernel_call(body, [shape(count // 2 * seq, wide)] * 2, [me], [*pieces, project])


def two_terms(row, rows):
    high, low = split_two(row)
    place = lax.broadcasted_iota(jnp.int32, (rows, row.shape[1]), 0)
    return jnp.where(place % 2 == 0, high, low).astype(BF16)


def add_two(left, right, tail=None):
    def body(left_ref, right_ref, out_ref):
        total = left_ref[...].astype(F32) + right_ref[...].astype(F32)
        out_ref[...] = total.astype(BF16)
        if tail is not None:
            means = total[tail : tail + 1, LANES:] + total[tail + 1 : tail + 2, LANES:]
            out_ref[tail:, LANES:] = two_terms(means, left.shape[0] - tail)

    return kernel_call(body, [shape(*left.shape)], [], [left, right])[0]


def attention_back(projected, head_half, row_mean, scale, seq, outs, width):
    grad_ref, mixed_ref, numbers_ref = outs
    rows, head = head_half.shape
    count = rows // seq
    root = math.sqrt(head)
    query, query_scale = normalize(projected[:, :head])
    key, key_scale = normalize(projected[:, head : 2 * head])
    query_half, key_half = query.astype(BF16), key.astype(BF16)
    value_half = projected[:, 2 * head :].astype(BF16)

    def each(function, *values):
        return jnp.concatenate(
            [function(*(v[r * seq : (r + 1) * seq] for v in values)) for r in range(count)], axis=0
        )

    def last(left, right):
        return dot(left, right, CONTRACT_LAST)

    def leading(left, right):
        return dot(left, right, CONTRACT_FIRST)

    powered = jnp.exp(each(last, query_half, key_half) / root)
    attention = powered / jnp.sum(powered, axis=-1, keepdims=True)
    attention_half = attention.astype(BF16)
    mixed_ref[...] = each(dot, attention_half, value_half).astype(BF16)
    prob_grad = each(last, head_half, value_half)
    value_grad = each(leading, attention_half, head_half).astype(BF16)
    score_grad = (
        attention * (prob_grad - jnp.sum(attention * prob_grad, axis=-1, keepdims=True)) / root
    ).astype(BF16)
    query_grad = norm_back(each(dot, score_grad, key_half), query, query_scale)
    key_grad = norm_back(each(leading, score_grad, query_half), key, key_scale)
    proj_grad = jnp.concatenate(
        [query_grad.astype(BF16), key_grad.astype(BF16), value_grad], axis=1
    )
    grad_ref[...] = proj_grad
    spread = proj_grad.astype(F32)
    offset = scale * jnp.sum(spread * row_mean, axis=-1, keepdims=True)
    slope = scale * (jnp.sum(spread * projected, axis=-1, keepdims=True) / width)
    lane = lax.broadcasted_iota(jnp.int32, (rows, LANES), 1)
    numbers_ref[...] = jnp.where(lane == 0, scale, jnp.where(lane == 1, offset, slope))
    return proj_grad, slope


def all_rows(half_refs, seq, half, columns):
    return jnp.concatenate([ref[: half * seq, columns] for ref in half_refs], axis=0).astype(F32)


def scale_column(half_refs, tick, ticks, seq, half):
    columns = []
    for ref in half_refs:
        facts = ref[half * seq :, :LANES].astype(F32)
        for block in range(half):
            row = 2 * (ticks * block + tick)
            columns.append(column(facts[row : row + 1] + facts[row + 1 : row + 2])[:seq, :1])
    return jnp.concatenate(columns, axis=0)


def row_means(half_refs, seq, half):
    facts = half_refs[0][half * seq :, LANES:].astype(F32)
    return facts[:1] + facts[1:2]


def attention_outs(rows, head):
    return [shape(rows, 3 * head), shape(rows, head), shape(rows, LANES, kind=F32)]


def below_parts(pieces, project, below, me):
    count, (_, seq, part) = len(pieces), pieces[0].shape
    wide, head = project.shape[1], below.shape[1]

    def body(me_ref, *refs):
        piece_refs, refs = refs[:count], refs[count:]
        project_ref, below_ref, rows_ref, product_ref, sums_ref = refs
        below = below_ref[...]
        for j in range(count):
            rows = block_rows(me_ref, j, count, seq)
            rows_ref[rows, :head] = dot(piece_refs[j][1], below)
            rows_ref[rows, head:] = dot(piece_refs[j][0], below)
        product_ref[...] = dot(project_ref[...], below, CONTRACT_FIRST)
        sums = jnp.sum(below.astype(F32), axis=0, keepdims=True)
        sums_ref[...] = jnp.broadcast_to(sums, sums_ref.shape)

    outs = [
        shape(count * seq, 2 * head, kind=F32),
        shape(wide, head, kind=F32),
        shape(8, head, kind=F32),
    ]
    return kernel_call(body, outs, [me], [*pieces, project, below])


def first_attention(halves, parts, tops, below, seq, half, head, ticks, me, first, width):
    rows, wide, count, runs = 2 * half * seq, 3 * head, 2 * half, len(tops)
    run = below.shape[0] // runs

    def body(me_ref, first_ref, *refs):
        mine, (rows_ref, product_ref, sums_ref), refs = refs[:2], refs[2:5], refs[5:]
        top_refs, (below_ref, *outs, head_ref) = refs[:runs], refs[runs:]
        scale = scale_column(mine, 0, ticks, seq, half)
        row_mean = row_means(mine, seq, half)
        proj_grad, slope = attention_back(
            all_rows(mine, seq, half, slice(0, wide)),
            all_rows(mine, seq, half, slice(wide, wide + head)).astype(BF16),
            row_mean,
            scale,
            seq,
            outs,
            width,
        )
        centered = [
            product_ref[start : start + LANES, :]
            - column(row_mean[:, start : start + LANES])[:, :1] * sums_ref[:1, :]
            for start in range(0, wide, LANES)
        ]
        across = dot(proj_grad, jnp.concatenate(centered, axis=0).astype(BF16))
        change = scale * across - slope * rows_ref[:, head:]
        heads = (rows_ref[:, :head] + change).astype(BF16)
        for parity in range(2):
            for block in range(half):
                replica = 2 * block + lax.rem(me_ref[0] + parity, 2)
                start = (parity * half + block) * seq
                place = pl.ds(pl.multiple_of(replica * seq, seq), seq)
                head_ref[place, :] = heads[start : start + seq]

        @pl.when(first_ref[0] == 1)
        def _():
            for block in range(count):
                replica = lax.bitwise_xor(me_ref[0], block)
                place = pl.ds(pl.multiple_of(replica * seq, seq), seq)
                head_ref[place, :] = sum(
                    dot(top_refs[a][block], below_ref[a * run : (a + 1) * run, :])
                    for a in range(runs)
                ).astype(BF16)

    outs = [*attention_outs(rows, head), shape(rows, head)]
    arrays = [*halves, *parts, *tops, below]
    return kernel_call(body, outs, [me, first], arrays)


def sum_heads(heads, seq, me):
    rows, head = heads[0].shape
    half = rows // seq // 2

    def body(me_ref, *refs):
        for parity in range(2):
            for block in range(half):
                replica = 2 * block + lax.rem(me_ref[0] + parity, 2)
                place = pl.ds(pl.multiple_of(replica * seq, seq), seq)
                total = sum(ref[place, :].astype(F32) for ref in refs[:-1])
                start = (parity * half + block) * seq
                refs[-1][start : start + seq, :] = total.astype(BF16)

    return kernel_call(body, [shape(rows, head)], [me], heads, cost=1)[0]


def later_attention(halves, facts, head_half, seq, half, head, ticks, width):
    rows = 2 * half * seq

    def body(*refs):
        mine, facts, (head_ref, *outs) = refs[:2], refs[2:4], refs[4:]
        attention_back(
            all_rows(mine, seq, half, slice(None)),
            head_ref[...],
            row_means(facts, seq, half),
            scale_column(facts, 1, ticks, seq, half),
            seq,
            outs,
            width,
        )

    arrays = [*halves, *facts, head_half]
    return kernel_call(body, attention_outs(rows, head), [], arrays, cost=1)


def input_gradient(hidden_grad, numbers, incoming, hidden):
    scale, offset, slope = (numbers[:, i : i + 1] for i in range(3))
    change = scale * hidden_grad - offset - slope * hidden.astype(F32)
    return (incoming.astype(F32) + change).astype(BF16)


def middle_step(grads, pieces, tops, project, me, first):
    count, (_, seq, part) = len(pieces), pieces[0].shape
    runs = len(tops)
    run = part // runs

    def body(me_ref, first_ref, *refs):
        top_refs, piece_refs, refs = refs[:runs], refs[runs : runs + count], refs[runs + count :]
        grad_ref, numbers_ref, project_ref, passed_ref, sems, wide_ref = refs
        is_first = first_ref[0] == 1

        @pl.when(is_first)
        def _():
            copies = []
            for j in range(count):
                block = lax.bitwise_xor(me_ref[0], replica_of(me_ref, j, count))
                for a in range(runs):
                    place = passed_ref.at[j, :, pl.ds(a * run, run)]
                    copies.append(
                        pltpu.make_async_copy(top_refs[a].at[block], place, sems.at[j, a])
                    )
                    copies[-1].start()
            for copy in copies:
                copy.wait()

        @pl.when(jnp.logical_not(is_first))
        def _():
            wide_ref[...] = dot(grad_ref[...], project_ref[...], CONTRACT_LAST)
            for j in range(count):
                rows = block_rows(me_ref, j, count, seq)
                hidden, incoming = piece_refs[j][0], piece_refs[j][1]
                passed_ref[j] = input_gradient(
                    wide_ref[rows, :], numbers_ref[rows, :], incoming, hidden
                )

    scratch = [
        pltpu.SemaphoreType.DMA((count, runs)),
        pltpu.VMEM((count * seq, part), F32),
    ]
    arrays = [*pieces, *grads, project]
    outs = [shape(count, seq, part)]
    return kernel_call(body, outs, [me, first], arrays, scratch, far=tops)[0]


def last_step(grads, received, pieces, project, me):
    count, (seq, part) = len(pieces), pieces[0].shape

    def body(me_ref, *refs):
        piece_refs, refs = refs[:count], refs[count:]
        grad_ref, numbers_ref, received_ref, project_ref, *outs, wide_ref = refs
        wide_ref[...] = dot(grad_ref[...], project_ref[...], CONTRACT_LAST)
        for j in range(count):
            rows = block_rows(me_ref, j, count, seq)
            outs[j][...] = input_gradient(
                wide_ref[rows, :], numbers_ref[rows, :], received_ref[j], piece_refs[j][...]
            )

    arrays = [*pieces, *grads, received, project]
    scratch = [pltpu.VMEM((count * seq, part), F32)]
    return list(kernel_call(body, [shape(seq, part)] * count, [me], arrays, scratch))


def weight_gradients(pieces, later, received, first_grads, later_grads, me):
    count, (_, seq, part) = len(pieces), pieces[0].shape
    wide, head = first_grads[0].shape[1], first_grads[1].shape[1]
    block = min(part, 256)

    def body(me_ref, *refs):
        piece_refs, later_refs, refs = refs[:count], refs[count : 2 * count], refs[2 * count :]
        received_ref, grad0, mixed0, grad1, mixed1, project_ref, output_ref = refs
        for start in range(0, part, block):
            columns = slice(start, start + block)
            project_sum, output_sum = 0.0, 0.0
            for j in range(count):
                rows = block_rows(me_ref, j, count, seq)
                value = dot(piece_refs[j][0, :, columns], grad0[rows, :], CONTRACT_FIRST)
                value += dot(later_refs[j][:, columns], grad1[rows, :], CONTRACT_FIRST)
                project_sum += value.astype(BF16).astype(F32)
                value = dot(piece_refs[j][1, :, columns], mixed0[rows, :], CONTRACT_FIRST)
                value += dot(received_ref[j, :, columns], mixed1[rows, :], CONTRACT_FIRST)
                output_sum += value.astype(BF16).astype(F32)
            project_ref[columns, :] = project_sum
            output_ref[columns, :] = output_sum

    outs = [shape(part, wide, kind=F32), shape(part, head, kind=F32)]
    arrays = [*pieces, *later, received, *first_grads, *later_grads]
    return kernel_call(body, outs, [me], arrays)


def join_features(pieces, me):
    count = len(pieces)
    seq, part = pieces[0].shape

    def body(me_ref, *refs):
        for j in range(count):
            owner = lax.rem(me_ref[0] + j, count)
            columns = pl.ds(pl.multiple_of(owner * part, LANES), part)
            refs[count][:, columns] = refs[j][...]

    return kernel_call(body, [shape(seq, part * count)], [me], pieces)[0]


def shift(value, steps):
    count = lax.axis_size("dp")
    if steps % count == 0:
        return value
    return lax.ppermute(value, "dp", [(i, (i + steps) % count) for i in range(count)])


def after(value, *earlier):
    return lax.optimization_barrier((value, *earlier))[0]


def down(value, steps=0):
    pipe, count = lax.axis_size("pipe"), lax.axis_size("dp")
    pairs = [
        (p * count + r, (p - 1) % pipe * count + (r + steps) % count)
        for p in range(pipe)
        for r in range(count)
    ]
    return lax.ppermute(value, BOTH, pairs)


def join_pieces(left, right):
    size = left.shape[0]

    def body(left_ref, right_ref, out_ref):
        out_ref[:size] = left_ref[...]
        out_ref[size:] = right_ref[...]

    outs = [shape(2 * size, *left.shape[1:])]
    return kernel_call(body, outs, [], [left, right])[0]


def toward_owner(blocks, bit):
    pipe, count = lax.axis_size("pipe"), lax.axis_size("dp")
    runs = pipe // count
    pairs = [
        (q * count + r, q * count + (r ^ bit))
        for q in range(pipe)
        for r in range(count)
        if (r ^ (q // runs)) % (2 * bit) == bit
    ]
    return lax.ppermute(blocks, BOTH, pairs)


def owner_to_first(blocks, run):
    pipe, count = lax.axis_size("pipe"), lax.axis_size("dp")
    runs = pipe // count
    return lax.ppermute(blocks, BOTH, [((runs * s + run) * count + s, s) for s in range(count)])


def exchanged(value, step):
    count = lax.axis_size("dp")
    return lax.ppermute(value, "dp", [(i, i ^ step) for i in range(count)])


def shards(section_inputs, arriving, top_grads, project_weights, output_weights):
    count = lax.axis_size("dp")
    pipe = lax.axis_size("pipe")
    me = lax.axis_index("dp")
    first = lax.axis_index("pipe") == 0
    _, ticks, seq, width = section_inputs.shape
    head = output_weights.shape[2]
    project, output = project_weights[0], output_weights[0]
    others, half = range(count), count // 2

    blocks, moved = top_grads, toward_owner(top_grads, 1)
    sent, scale = first_pieces(section_inputs[0], arriving[0], me, count)
    pieces = [shift(sent[j], j) for j in others]
    later_sent, later_scale = later_pieces(section_inputs[0], me, count)
    blocks = join_pieces(after(blocks, later_scale), moved)
    bit = 2
    while bit < count // 2:
        blocks = join_pieces(blocks, toward_owner(blocks, bit))
        bit *= 2
    moved = toward_owner(blocks, bit) if bit < count else None

    mine, other = first_partials(
        pieces, [scale, later_scale], after(project, blocks), output, me, width
    )
    below = lax.ppermute(
        after(output, other), "pipe", [(p, (p + 1) % pipe) for p in range(pipe)]
    )
    later_sent = after(tuple(later_sent), other)
    later = [shift(later_sent[j], j) for j in others]
    early = [later[j] for j in [2] if j < count]
    total = add_two(after(mine, below, *early), exchanged(other, 1), half * seq)
    if moved is not None:
        blocks = join_pieces(after(blocks, total), moved)
    tops = [owner_to_first(blocks, run) for run in range(pipe // count)]
    later_mine, later_other = later_partials(later, after(project, total), me)
    parts = below_parts(pieces, project, below, me)
    step = 2
    while step < count:
        received = exchanged(total, step)
        total = add_two(after(total, later_other), received, half * seq)
        step *= 2
    halves = [total, exchanged(total, 1)]
    later_total = add_two(later_mine, exchanged(later_other, 1))
    halves[0] = after(halves[0], later_total)
    later_parts, step = [later_total], 2
    while step < count:
        later_parts = [later_total, exchanged(later_total, step)]
        later_total = add_two(*later_parts)
        step *= 2

    *first_grads, heads = first_attention(
        halves, parts, tops, below, seq, half, head, ticks, me, first, width
    )
    heads = [down(heads, j) for j in others]
    later_halves = [later_total, exchanged(later_total, 1)]
    passed = middle_step([first_grads[0], first_grads[2]], pieces, tops, project, me, first)
    received = down(after(passed, later_parts[-1]))
    head_half = sum_heads(heads, seq, me)
    later_grads = later_attention(
        later_halves, halves, head_half, seq, half, head, ticks, width
    )
    back = last_step([later_grads[0], later_grads[2]], received, later, project, me)
    mixed = after(later_grads[1], back[0])
    back = [shift(back[j], -j) for j in others]
    project_grads, output_grads = weight_gradients(
        pieces, later, received, first_grads[:2], [later_grads[0], mixed], me
    )
    passed_back = join_features(back, me)
    return (project_grads[None], output_grads[None], passed_back[None])


def solution(mesh):
    in_specs = (
        P("pipe", None, "dp", None),
        P("pipe", "dp", None),
        P(None, "dp", "pipe"),
        P("pipe", "dp", None),
        P("pipe", "dp", None),
    )
    out_specs = (P("pipe", "dp", None), P("pipe", "dp", None), P("pipe", "dp", None))
    return jax.shard_map(shards, mesh=mesh, in_specs=in_specs, out_specs=out_specs, check_vma=False)
```

```python
import functools
import math

import jax
import jax.numpy as jnp
from jax import lax
from jax.experimental import pallas as pl
from jax.experimental.pallas import tpu as pltpu
from jax.sharding import PartitionSpec as P

EPSILON = 1e-06
CONTRACT_FIRST = (((0,), (0,)), ((), ()))
CONTRACT_LAST = (((1,), (1,)), ((), ()))
F32 = jnp.float32
BF16 = jnp.bfloat16
ROW_TILE = 16
LANES = 128
BOTH = ("pipe", "dp")


def shape(*dims, kind=BF16):
    return jax.ShapeDtypeStruct(dims, kind)


def kernel_call(body, outs, scalars, arrays, scratch=(), far=(), cost=1):
    return pl.pallas_call(
        body,
        out_shape=tuple(outs),
        in_specs=[pl.BlockSpec(memory_space=pltpu.SMEM)] * len(scalars)
        + [pl.BlockSpec(memory_space=pl.ANY)] * len(far)
        + [pl.BlockSpec(memory_space=pltpu.VMEM)] * len(arrays),
        out_specs=tuple(pl.BlockSpec(memory_space=pltpu.VMEM) for _ in outs),
        scratch_shapes=list(scratch),
        compiler_params=pltpu.CompilerParams(vmem_limit_bytes=24 * 1024 * 1024),
        cost_estimate=pl.CostEstimate(flops=1, bytes_accessed=cost, transcendentals=0),
    )(*[s.reshape(1).astype(jnp.int32) for s in scalars], *far, *arrays)


def dot(left, right, contract=(((1,), (0,)), ((), ()))):
    return lax.dot_general(left, right, contract, preferred_element_type=F32)


def normalize(values):
    centered = values - jnp.mean(values, axis=-1, keepdims=True)
    inverse = lax.rsqrt(jnp.mean(centered * centered, axis=-1, keepdims=True) + EPSILON)
    return (centered * inverse, inverse)


def norm_back(gradient, normed, inverse):
    centered = gradient - jnp.mean(gradient, axis=-1, keepdims=True)
    return inverse * (centered - normed * jnp.mean(gradient * normed, axis=-1, keepdims=True))


def column(row):
    return jnp.broadcast_to(row, (LANES, LANES)).T


def as_row(column):
    seq = column.shape[0]
    if seq < LANES:
        column = jnp.concatenate([column, jnp.zeros((LANES - seq, LANES), F32)], axis=0)
    return column.T[:1]


def split_two(value):
    high = value.astype(BF16).astype(F32)
    return high, value - high


def replica_of(me_ref, j, count):
    return lax.rem(me_ref[0] + count - j, count)


def block_rows(me_ref, j, count, seq):
    block = replica_of(me_ref, j, count) // 2 + (j % 2) * (count // 2)
    return pl.ds(pl.multiple_of(block * seq, seq), seq)


def first_pieces(inputs, arriving, me, count):
    seq, width = arriving.shape
    part = width // count

    def body(me_ref, x_ref, arriving_ref, *refs):
        outs, (scale_ref, hidden_ref) = refs[:count], refs[count:]
        for row in range(0, seq, ROW_TILE):
            rows = slice(row, row + ROW_TILE)
            normed, inverse = normalize(x_ref[0, rows, :].astype(F32))
            hidden_ref[rows, :] = normed.astype(BF16)
            scale_ref[rows, :] = jnp.broadcast_to(inverse, (ROW_TILE, LANES))
        for j in range(count):
            owner = lax.rem(me_ref[0] + j, count)
            columns = pl.ds(pl.multiple_of(owner * part, LANES), part)
            outs[j][0] = hidden_ref[:, columns]
            outs[j][1] = arriving_ref[:, columns]

    outs = [shape(2, seq, part)] * count + [shape(seq, LANES, kind=F32)]
    scratch = [pltpu.VMEM((seq, width), BF16)]
    result = kernel_call(body, outs, [me], [inputs, arriving], scratch)
    return list(result[:count]), result[count]


def later_pieces(inputs, me, count):
    _, seq, width = inputs.shape
    part = width // count

    def body(me_ref, x_ref, *refs):
        outs, (scale_ref, hidden_ref) = refs[:count], refs[count:]
        for row in range(0, seq, ROW_TILE):
            rows = slice(row, row + ROW_TILE)
            normed, inverse = normalize(x_ref[1, rows, :].astype(F32))
            hidden_ref[rows, :] = normed.astype(BF16)
            scale_ref[rows, :] = jnp.broadcast_to(inverse, (ROW_TILE, LANES))
        for j in range(count):
            owner = lax.rem(me_ref[0] + j, count)
            columns = pl.ds(pl.multiple_of(owner * part, LANES), part)
            outs[j][...] = hidden_ref[:, columns]

    outs = [shape(seq, part)] * count + [shape(seq, LANES, kind=F32)]
    scratch = [pltpu.VMEM((seq, width), BF16)]
    result = kernel_call(body, outs, [me], [inputs], scratch)
    return list(result[:count]), result[count]


def first_partials(pieces, scales, project, output, me, width):
    count = len(pieces)
    _, seq, part = pieces[0].shape
    wide, head = project.shape[1], output.shape[1]
    half, ticks = count // 2, len(scales)
    extra = -(-2 * ticks * half // ROW_TILE) * ROW_TILE

    def body(me_ref, *refs):
        piece_refs, refs = refs[:count], refs[count:]
        scale_refs, (project_ref, output_ref, *outs) = refs[:ticks], refs[ticks:]
        project = project_ref[...]
        hidden = jnp.concatenate([ref[0] for ref in piece_refs], axis=0)
        projected = dot(hidden, project).astype(BF16)
        incoming = jnp.concatenate([ref[1] for ref in piece_refs], axis=0)
        heads = dot(incoming, output_ref[...]).astype(BF16)
        for j in range(count):
            out_ref, rows = outs[j % 2], half_rows(me_ref, j, count, seq)
            place = slice(j * seq, (j + 1) * seq)
            out_ref[rows, :wide] = projected[place]
            out_ref[rows, wide:] = heads[place]
        sums = jnp.sum(project.astype(F32), axis=0, keepdims=True) / width
        place = lax.broadcasted_iota(jnp.int32, (extra, LANES), 0) - 2 * ticks * (me_ref[0] // 2)
        facts = jnp.zeros((extra, LANES), F32)
        for t in range(ticks):
            for index, value in enumerate(split_two(as_row(scale_refs[t][...]))):
                facts = jnp.where(place == 2 * t + index, value, facts)
        for out_ref, lanes in zip(outs, (facts, jnp.zeros((extra, LANES), F32))):
            out_ref[half * seq :, :LANES] = lanes.astype(BF16)
            out_ref[half * seq :, LANES:] = two_terms(sums, extra)

    outs = [shape(half * seq + extra, wide + head)] * 2
    return kernel_call(body, outs, [me], [*pieces, *scales, project, output])


def half_rows(me_ref, j, count, seq):
    block = replica_of(me_ref, j, count) // 2
    return pl.ds(pl.multiple_of(block * seq, seq), seq)


def later_partials(pieces, project, me):
    count = len(pieces)
    seq = pieces[0].shape[0]
    wide = project.shape[1]

    def body(me_ref, *refs):
        piece_refs, (project_ref, *outs) = refs[:count], refs[count:]
        hidden = jnp.concatenate([ref[...] for ref in piece_refs], axis=0)
        value = dot(hidden, project_ref[...]).astype(BF16)
        for j in range(count):
            rows = half_rows(me_ref, j, count, seq)
            outs[j % 2][rows, :] = value[j * seq : (j + 1) * seq]

    return kernel_call(body, [shape(count // 2 * seq, wide)] * 2, [me], [*pieces, project])


def two_terms(row, rows):
    high, low = split_two(row)
    place = lax.broadcasted_iota(jnp.int32, (rows, row.shape[1]), 0)
    return jnp.where(place % 2 == 0, high, low).astype(BF16)


def add_two(left, right, tail=None):
    def body(left_ref, right_ref, out_ref):
        total = left_ref[...].astype(F32) + right_ref[...].astype(F32)
        out_ref[...] = total.astype(BF16)
        if tail is not None:
            means = total[tail : tail + 1, LANES:] + total[tail + 1 : tail + 2, LANES:]
            out_ref[tail:, LANES:] = two_terms(means, left.shape[0] - tail)

    return kernel_call(body, [shape(*left.shape)], [], [left, right])[0]


def each(function, seq, *values):
    count = values[0].shape[0] // seq
    return jnp.concatenate(
        [function(*(v[r * seq : (r + 1) * seq] for v in values)) for r in range(count)], axis=0
    )


def dot_last(left, right):
    return dot(left, right, CONTRACT_LAST)


def dot_first(left, right):
    return dot(left, right, CONTRACT_FIRST)


def attention_front(projected, seq, mixed_ref):
    head = projected.shape[1] // 3
    query, query_scale = normalize(projected[:, :head])
    key, key_scale = normalize(projected[:, head : 2 * head])
    value_half = projected[:, 2 * head :].astype(BF16)
    scores = each(dot_last, seq, query.astype(BF16), key.astype(BF16))
    powered = jnp.exp(scores / math.sqrt(head))
    attention = powered / jnp.sum(powered, axis=-1, keepdims=True)
    mixed_ref[...] = each(dot, seq, attention.astype(BF16), value_half).astype(BF16)
    return query, key, attention, value_half, query_scale, key_scale


def attention_back(projected, front, head_half, row_mean, scale, seq, outs, width):
    query, key, attention, value_half, query_scale, key_scale = front
    grad_ref, numbers_ref = outs
    rows, head = head_half.shape
    root = math.sqrt(head)
    prob_grad = each(dot_last, seq, head_half, value_half)
    value_grad = each(dot_first, seq, attention.astype(BF16), head_half).astype(BF16)
    score_grad = (
        attention * (prob_grad - jnp.sum(attention * prob_grad, axis=-1, keepdims=True)) / root
    ).astype(BF16)
    query_grad = norm_back(each(dot, seq, score_grad, key.astype(BF16)), query, query_scale)
    key_grad = norm_back(each(dot_first, seq, score_grad, query.astype(BF16)), key, key_scale)
    proj_grad = jnp.concatenate(
        [query_grad.astype(BF16), key_grad.astype(BF16), value_grad], axis=1
    )
    grad_ref[...] = proj_grad
    spread = proj_grad.astype(F32)
    offset = scale * jnp.sum(spread * row_mean, axis=-1, keepdims=True)
    slope = scale * (jnp.sum(spread * projected, axis=-1, keepdims=True) / width)
    lane = lax.broadcasted_iota(jnp.int32, (rows, LANES), 1)
    numbers_ref[...] = jnp.where(lane == 0, scale, jnp.where(lane == 1, offset, slope))
    return proj_grad, slope


def all_rows(half_refs, seq, half, columns):
    return jnp.concatenate([ref[: half * seq, columns] for ref in half_refs], axis=0).astype(F32)


def scale_column(half_refs, tick, ticks, seq, half):
    columns = []
    for ref in half_refs:
        facts = ref[half * seq :, :LANES].astype(F32)
        for block in range(half):
            row = 2 * (ticks * block + tick)
            columns.append(column(facts[row : row + 1] + facts[row + 1 : row + 2])[:seq, :1])
    return jnp.concatenate(columns, axis=0)


def row_means(half_refs, seq, half):
    facts = half_refs[0][half * seq :, LANES:].astype(F32)
    return facts[:1] + facts[1:2]


def attention_outs(rows, head):
    return [shape(rows, 3 * head), shape(rows, head), shape(rows, LANES, kind=F32)]


def below_parts(pieces, project, below, me):
    count, (_, seq, part) = len(pieces), pieces[0].shape
    wide, head = project.shape[1], below.shape[1]

    def body(me_ref, *refs):
        piece_refs, refs = refs[:count], refs[count:]
        project_ref, below_ref, rows_ref, product_ref, sums_ref = refs
        below = below_ref[...]
        for j in range(count):
            rows = block_rows(me_ref, j, count, seq)
            rows_ref[rows, :head] = dot(piece_refs[j][1], below)
            rows_ref[rows, head:] = dot(piece_refs[j][0], below)
        product_ref[...] = dot(project_ref[...], below, CONTRACT_FIRST)
        sums = jnp.sum(below.astype(F32), axis=0, keepdims=True)
        sums_ref[...] = jnp.broadcast_to(sums, sums_ref.shape)

    outs = [
        shape(count * seq, 2 * head, kind=F32),
        shape(wide, head, kind=F32),
        shape(8, head, kind=F32),
    ]
    return kernel_call(body, outs, [me], [*pieces, project, below])


def first_attention(halves, parts, tops, below, seq, half, head, ticks, me, first, width):
    rows, wide, count, runs = 2 * half * seq, 3 * head, 2 * half, len(tops)
    run = below.shape[0] // runs

    def body(me_ref, first_ref, *refs):
        mine, (rows_ref, product_ref, sums_ref), refs = refs[:2], refs[2:5], refs[5:]
        top_refs, (below_ref, *outs, head_ref) = refs[:runs], refs[runs:]
        scale = scale_column(mine, 0, ticks, seq, half)
        row_mean = row_means(mine, seq, half)
        projected = all_rows(mine, seq, half, slice(0, wide))
        grad_ref, mixed_ref, numbers_ref = outs
        proj_grad, slope = attention_back(
            projected,
            attention_front(projected, seq, mixed_ref),
            all_rows(mine, seq, half, slice(wide, wide + head)).astype(BF16),
            row_mean,
            scale,
            seq,
            (grad_ref, numbers_ref),
            width,
        )
        centered = [
            product_ref[start : start + LANES, :]
            - column(row_mean[:, start : start + LANES])[:, :1] * sums_ref[:1, :]
            for start in range(0, wide, LANES)
        ]
        across = dot(proj_grad, jnp.concatenate(centered, axis=0).astype(BF16))
        change = scale * across - slope * rows_ref[:, head:]
        heads = (rows_ref[:, :head] + change).astype(BF16)
        for parity in range(2):
            for block in range(half):
                replica = 2 * block + lax.rem(me_ref[0] + parity, 2)
                start = (parity * half + block) * seq
                place = pl.ds(pl.multiple_of(replica * seq, seq), seq)
                head_ref[place, :] = heads[start : start + seq]

        @pl.when(first_ref[0] == 1)
        def _():
            for block in range(count):
                replica = lax.bitwise_xor(me_ref[0], block)
                place = pl.ds(pl.multiple_of(replica * seq, seq), seq)
                head_ref[place, :] = sum(
                    dot(top_refs[a][block], below_ref[a * run : (a + 1) * run, :])
                    for a in range(runs)
                ).astype(BF16)

    outs = [*attention_outs(rows, head), shape(rows, head)]
    arrays = [*halves, *parts, *tops, below]
    return kernel_call(body, outs, [me, first], arrays)


def sum_heads(heads, received, seq, me):
    rows, head = heads[0].shape
    count = rows // seq
    half, part = count // 2, received.shape[2] - head

    def body(me_ref, *refs):
        *head_refs, received_ref, out_ref = refs
        for parity in range(2):
            for block in range(half):
                replica = 2 * block + lax.rem(me_ref[0] + parity, 2)
                place = pl.ds(pl.multiple_of(replica * seq, seq), seq)
                total = sum(ref[place, :].astype(F32) for ref in head_refs)
                piece = lax.rem(me_ref[0] + count - replica, count)
                total += received_ref[piece, :, part:].astype(F32)
                start = (parity * half + block) * seq
                out_ref[start : start + seq, :] = total.astype(BF16)

    return kernel_call(body, [shape(rows, head)], [me], [*heads, received])[0]


def later_front(halves, facts, seq, half, head, ticks):
    rows = 2 * half * seq

    def body(*refs):
        mine, facts, outs = refs[:2], refs[2:4], refs[4:]
        mixed_ref, projected_ref, query_ref, key_ref, attention_ref, value_ref, scales_ref = outs
        projected = all_rows(mine, seq, half, slice(None))
        query, key, attention, value_half, *scales = attention_front(projected, seq, mixed_ref)
        projected_ref[...] = projected
        query_ref[...], key_ref[...] = query, key
        attention_ref[...], value_ref[...] = attention, value_half
        scales.append(scale_column(facts, 1, ticks, seq, half))
        for place, scale in enumerate(scales):
            scales_ref[place] = jnp.broadcast_to(scale, (rows, LANES))

    outs = [
        shape(rows, head),
        shape(rows, 3 * head, kind=F32),
        shape(rows, head, kind=F32),
        shape(rows, head, kind=F32),
        shape(rows, seq, kind=F32),
        shape(rows, head),
        shape(3, rows, LANES, kind=F32),
    ]
    return kernel_call(body, outs, [], [*halves, *facts])


def later_attention(front, facts, head_half, seq, half, head, width):
    rows = 2 * half * seq

    def body(*refs):
        projected_ref, query_ref, key_ref, attention_ref, value_ref, scales_ref = refs[:6]
        facts, (head_ref, *outs) = refs[6:8], refs[8:]
        scales = [scales_ref[place, :, :1] for place in range(3)]
        front = [query_ref[...], key_ref[...], attention_ref[...], value_ref[...], *scales[:2]]
        attention_back(
            projected_ref[...],
            front,
            head_ref[...],
            row_means(facts, seq, half),
            scales[2],
            seq,
            outs,
            width,
        )

    arrays = [*front, *facts, head_half]
    outs = [shape(rows, 3 * head), shape(rows, LANES, kind=F32)]
    return kernel_call(body, outs, [], arrays)


def input_gradient(hidden_grad, numbers, incoming, hidden):
    scale, offset, slope = (numbers[:, i : i + 1] for i in range(3))
    change = scale * hidden_grad - offset - slope * hidden.astype(F32)
    return (incoming.astype(F32) + change).astype(BF16)


def middle_step(grads, heads, pieces, tops, project, me, first):
    count, (_, seq, part) = len(pieces), pieces[0].shape
    runs = len(tops)
    run = part // runs

    def body(me_ref, first_ref, *refs):
        top_refs, piece_refs, refs = refs[:runs], refs[runs : runs + count], refs[runs + count :]
        grad_ref, numbers_ref, head_ref, project_ref, passed_ref, sems, wide_ref = refs
        is_first = first_ref[0] == 1
        for j in range(count):
            place = pl.ds(pl.multiple_of(replica_of(me_ref, j, count) * seq, seq), seq)
            passed_ref[j, :, part:] = head_ref[place, :]

        @pl.when(is_first)
        def _():
            copies = []
            for j in range(count):
                block = lax.bitwise_xor(me_ref[0], replica_of(me_ref, j, count))
                for a in range(runs):
                    place = passed_ref.at[j, :, pl.ds(a * run, run)]
                    copies.append(
                        pltpu.make_async_copy(top_refs[a].at[block], place, sems.at[j, a])
                    )
                    copies[-1].start()
            for copy in copies:
                copy.wait()

        @pl.when(jnp.logical_not(is_first))
        def _():
            wide_ref[...] = dot(grad_ref[...], project_ref[...], CONTRACT_LAST)
            for j in range(count):
                rows = block_rows(me_ref, j, count, seq)
                hidden, incoming = piece_refs[j][0], piece_refs[j][1]
                passed_ref[j, :, :part] = input_gradient(
                    wide_ref[rows, :], numbers_ref[rows, :], incoming, hidden
                )

    scratch = [
        pltpu.SemaphoreType.DMA((count, runs)),
        pltpu.VMEM((count * seq, part), F32),
    ]
    arrays = [*pieces, *grads, heads, project]
    outs = [shape(count, seq, part + heads.shape[1])]
    return kernel_call(body, outs, [me, first], arrays, scratch, far=tops)[0]


def last_step(grads, received, pieces, project, me):
    count, (seq, part) = len(pieces), pieces[0].shape

    def body(me_ref, *refs):
        piece_refs, refs = refs[:count], refs[count:]
        grad_ref, numbers_ref, received_ref, project_ref, *outs, wide_ref = refs
        wide_ref[...] = dot(grad_ref[...], project_ref[...], CONTRACT_LAST)
        for j in range(count):
            rows = block_rows(me_ref, j, count, seq)
            outs[j][...] = input_gradient(
                wide_ref[rows, :], numbers_ref[rows, :], received_ref[j, :, :part], piece_refs[j][...]
            )

    arrays = [*pieces, *grads, received, project]
    scratch = [pltpu.VMEM((count * seq, part), F32)]
    return list(kernel_call(body, [shape(seq, part)] * count, [me], arrays, scratch))


def weight_gradients(pieces, later, received, first_grads, later_grads, me):
    count, (_, seq, part) = len(pieces), pieces[0].shape
    wide, head = first_grads[0].shape[1], first_grads[1].shape[1]
    block = min(part, 256)

    def body(me_ref, *refs):
        piece_refs, later_refs, refs = refs[:count], refs[count : 2 * count], refs[2 * count :]
        received_ref, grad0, mixed0, grad1, mixed1, project_ref, output_ref = refs
        for start in range(0, part, block):
            columns = slice(start, start + block)
            project_sum, output_sum = 0.0, 0.0
            for j in range(count):
                rows = block_rows(me_ref, j, count, seq)
                value = dot(piece_refs[j][0, :, columns], grad0[rows, :], CONTRACT_FIRST)
                value += dot(later_refs[j][:, columns], grad1[rows, :], CONTRACT_FIRST)
                project_sum += value.astype(BF16).astype(F32)
                value = dot(piece_refs[j][1, :, columns], mixed0[rows, :], CONTRACT_FIRST)
                value += dot(received_ref[j, :, columns], mixed1[rows, :], CONTRACT_FIRST)
                output_sum += value.astype(BF16).astype(F32)
            project_ref[columns, :] = project_sum
            output_ref[columns, :] = output_sum

    outs = [shape(part, wide, kind=F32), shape(part, head, kind=F32)]
    arrays = [*pieces, *later, received, *first_grads, *later_grads]
    return kernel_call(body, outs, [me], arrays)


def join_features(pieces, me):
    count = len(pieces)
    seq, part = pieces[0].shape

    def body(me_ref, *refs):
        for j in range(count):
            owner = lax.rem(me_ref[0] + j, count)
            columns = pl.ds(pl.multiple_of(owner * part, LANES), part)
            refs[count][:, columns] = refs[j][...]

    return kernel_call(body, [shape(seq, part * count)], [me], pieces)[0]


def shift(value, steps):
    count = lax.axis_size("dp")
    if steps % count == 0:
        return value
    return lax.ppermute(value, "dp", [(i, (i + steps) % count) for i in range(count)])


def after(value, *earlier):
    return lax.optimization_barrier((value, *earlier))[0]


def down(value, steps=0):
    pipe, count = lax.axis_size("pipe"), lax.axis_size("dp")
    pairs = [
        (p * count + r, (p - 1) % pipe * count + (r + steps) % count)
        for p in range(pipe)
        for r in range(count)
    ]
    return lax.ppermute(value, BOTH, pairs)


def join_pieces(left, right):
    size = left.shape[0]

    def body(left_ref, right_ref, out_ref):
        out_ref[:size] = left_ref[...]
        out_ref[size:] = right_ref[...]

    outs = [shape(2 * size, *left.shape[1:])]
    return kernel_call(body, outs, [], [left, right])[0]


def toward_owner(blocks, bit):
    pipe, count = lax.axis_size("pipe"), lax.axis_size("dp")
    runs = pipe // count
    pairs = [
        (q * count + r, q * count + (r ^ bit))
        for q in range(pipe)
        for r in range(count)
        if (r ^ (q // runs)) % (2 * bit) == bit
    ]
    return lax.ppermute(blocks, BOTH, pairs)


def owner_to_first(blocks, run):
    pipe, count = lax.axis_size("pipe"), lax.axis_size("dp")
    runs = pipe // count
    return lax.ppermute(blocks, BOTH, [((runs * s + run) * count + s, s) for s in range(count)])


def exchanged(value, step):
    count = lax.axis_size("dp")
    return lax.ppermute(value, "dp", [(i, i ^ step) for i in range(count)])


def shards(section_inputs, arriving, top_grads, project_weights, output_weights):
    count = lax.axis_size("dp")
    pipe = lax.axis_size("pipe")
    me = lax.axis_index("dp")
    first = lax.axis_index("pipe") == 0
    _, ticks, seq, width = section_inputs.shape
    head = output_weights.shape[2]
    project, output = project_weights[0], output_weights[0]
    others, half = range(count), count // 2

    blocks, moved = top_grads, toward_owner(top_grads, 1)
    sent, scale = first_pieces(section_inputs[0], arriving[0], me, count)
    pieces = [shift(sent[j], j) for j in others]
    later_sent, later_scale = later_pieces(section_inputs[0], me, count)
    blocks = join_pieces(after(blocks, later_scale), moved)
    bit = 2
    while bit < count // 2:
        blocks = join_pieces(blocks, toward_owner(blocks, bit))
        bit *= 2
    moved = toward_owner(blocks, bit) if bit < count else None

    mine, other = first_partials(
        pieces, [scale, later_scale], after(project, blocks), output, me, width
    )
    below = lax.ppermute(
        after(output, other), "pipe", [(p, (p + 1) % pipe) for p in range(pipe)]
    )
    later_sent = after(tuple(later_sent), other)
    later = [shift(later_sent[j], j) for j in others]
    early = [later[j] for j in [2] if j < count]
    total = add_two(after(mine, below, *early), exchanged(other, 1), half * seq)
    if moved is not None:
        blocks = join_pieces(after(blocks, total), moved)
    tops = [owner_to_first(blocks, run) for run in range(pipe // count)]
    later_mine, later_other = later_partials(later, after(project, total), me)
    parts = below_parts(pieces, project, below, me)
    step = 2
    while step < count:
        received = exchanged(total, step)
        total = add_two(after(total, later_other), received, half * seq)
        step *= 2
    halves = [total, exchanged(total, 1)]
    later_total = add_two(later_mine, exchanged(later_other, 1))
    halves[0] = after(halves[0], later_total)
    later_parts, step = [later_total], 2
    while step < count:
        later_parts = [later_total, exchanged(later_total, step)]
        later_total = add_two(*later_parts)
        step *= 2

    *first_grads, heads = first_attention(
        halves, parts, tops, below, seq, half, head, ticks, me, first, width
    )
    moved_heads = [down(heads, j) for j in others[1:]]
    later_halves = [later_total, exchanged(later_total, 1)]
    passed = middle_step(
        [first_grads[0], first_grads[2]], heads, pieces, tops, project, me, first
    )
    received = down(after(passed, later_parts[-1]))
    mixed, *front = later_front(later_halves, halves, seq, half, head, ticks)
    moved_heads[0] = after(moved_heads[0], mixed)
    head_half = sum_heads(moved_heads, received, seq, me)
    later_grads = later_attention(front, halves, head_half, seq, half, head, width)
    back = last_step(later_grads, received, later, project, me)
    mixed = after(mixed, back[0])
    back = [shift(back[j], -j) for j in others]
    project_grads, output_grads = weight_gradients(
        pieces, later, received, first_grads[:2], [later_grads[0], mixed], me
    )
    passed_back = join_features(back, me)
    return (project_grads[None], output_grads[None], passed_back[None])


def solution(mesh):
    in_specs = (
        P("pipe", None, "dp", None),
        P("pipe", "dp", None),
        P(None, "dp", "pipe"),
        P("pipe", "dp", None),
        P("pipe", "dp", None),
    )
    out_specs = (P("pipe", "dp", None), P("pipe", "dp", None), P("pipe", "dp", None))
    return jax.shard_map(shards, mesh=mesh, in_specs=in_specs, out_specs=out_specs, check_vma=False)
```

```python
import functools
import math

import jax
import jax.numpy as jnp
from jax import lax
from jax.experimental import pallas as pl
from jax.experimental.pallas import tpu as pltpu
from jax.sharding import PartitionSpec as P

EPSILON = 1e-06
CONTRACT_FIRST = (((0,), (0,)), ((), ()))
CONTRACT_LAST = (((1,), (1,)), ((), ()))
F32 = jnp.float32
BF16 = jnp.bfloat16
ROW_TILE = 16
LANES = 128
BOTH = ("pipe", "dp")


def shape(*dims, kind=BF16):
    return jax.ShapeDtypeStruct(dims, kind)


def kernel_call(body, outs, scalars, arrays, scratch=(), far=(), cost=1):
    return pl.pallas_call(
        body,
        out_shape=tuple(outs),
        in_specs=[pl.BlockSpec(memory_space=pltpu.SMEM)] * len(scalars)
        + [pl.BlockSpec(memory_space=pl.ANY)] * len(far)
        + [pl.BlockSpec(memory_space=pltpu.VMEM)] * len(arrays),
        out_specs=tuple(pl.BlockSpec(memory_space=pltpu.VMEM) for _ in outs),
        scratch_shapes=list(scratch),
        compiler_params=pltpu.CompilerParams(vmem_limit_bytes=24 * 1024 * 1024),
        cost_estimate=pl.CostEstimate(flops=1, bytes_accessed=cost, transcendentals=0),
    )(*[s.reshape(1).astype(jnp.int32) for s in scalars], *far, *arrays)


def dot(left, right, contract=(((1,), (0,)), ((), ()))):
    return lax.dot_general(left, right, contract, preferred_element_type=F32)


def normalize(values):
    centered = values - jnp.mean(values, axis=-1, keepdims=True)
    inverse = lax.rsqrt(jnp.mean(centered * centered, axis=-1, keepdims=True) + EPSILON)
    return (centered * inverse, inverse)


def norm_back(gradient, normed, inverse):
    centered = gradient - jnp.mean(gradient, axis=-1, keepdims=True)
    return inverse * (centered - normed * jnp.mean(gradient * normed, axis=-1, keepdims=True))


def column(row):
    return jnp.broadcast_to(row, (LANES, LANES)).T


def as_row(column):
    seq = column.shape[0]
    if seq < LANES:
        column = jnp.concatenate([column, jnp.zeros((LANES - seq, LANES), F32)], axis=0)
    return column.T[:1]


def split_two(value):
    high = value.astype(BF16).astype(F32)
    return high, value - high


def replica_of(me_ref, j, count):
    return lax.rem(me_ref[0] + count - j, count)


def block_rows(me_ref, j, count, seq):
    block = replica_of(me_ref, j, count) // 2 + (j % 2) * (count // 2)
    return pl.ds(pl.multiple_of(block * seq, seq), seq)


def first_pieces(inputs, arriving, me, count):
    seq, width = arriving.shape
    part = width // count

    def body(me_ref, x_ref, arriving_ref, *refs):
        outs, (scale_ref, hidden_ref) = refs[:count], refs[count:]
        for row in range(0, seq, ROW_TILE):
            rows = slice(row, row + ROW_TILE)
            normed, inverse = normalize(x_ref[0, rows, :].astype(F32))
            hidden_ref[rows, :] = normed.astype(BF16)
            scale_ref[rows, :] = jnp.broadcast_to(inverse, (ROW_TILE, LANES))
        for j in range(count):
            owner = lax.rem(me_ref[0] + j, count)
            columns = pl.ds(pl.multiple_of(owner * part, LANES), part)
            outs[j][0] = hidden_ref[:, columns]
            outs[j][1] = arriving_ref[:, columns]

    outs = [shape(2, seq, part)] * count + [shape(seq, LANES, kind=F32)]
    scratch = [pltpu.VMEM((seq, width), BF16)]
    result = kernel_call(body, outs, [me], [inputs, arriving], scratch)
    return list(result[:count]), result[count]


def later_pieces(inputs, me, count):
    _, seq, width = inputs.shape
    part = width // count

    def body(me_ref, x_ref, *refs):
        outs, (scale_ref, hidden_ref) = refs[:count], refs[count:]
        for row in range(0, seq, ROW_TILE):
            rows = slice(row, row + ROW_TILE)
            normed, inverse = normalize(x_ref[1, rows, :].astype(F32))
            hidden_ref[rows, :] = normed.astype(BF16)
            scale_ref[rows, :] = jnp.broadcast_to(inverse, (ROW_TILE, LANES))
        for j in range(count):
            owner = lax.rem(me_ref[0] + j, count)
            columns = pl.ds(pl.multiple_of(owner * part, LANES), part)
            outs[j][...] = hidden_ref[:, columns]

    outs = [shape(seq, part)] * count + [shape(seq, LANES, kind=F32)]
    scratch = [pltpu.VMEM((seq, width), BF16)]
    result = kernel_call(body, outs, [me], [inputs], scratch)
    return list(result[:count]), result[count]


def first_partials(pieces, scales, project, output, me, width):
    count = len(pieces)
    _, seq, part = pieces[0].shape
    wide, head = project.shape[1], output.shape[1]
    half, ticks = count // 2, len(scales)
    extra = -(-2 * ticks * half // ROW_TILE) * ROW_TILE

    def body(me_ref, *refs):
        piece_refs, refs = refs[:count], refs[count:]
        scale_refs, (project_ref, output_ref, *outs) = refs[:ticks], refs[ticks:]
        project = project_ref[...]
        hidden = jnp.concatenate([ref[0] for ref in piece_refs], axis=0)
        projected = dot(hidden, project).astype(BF16)
        incoming = jnp.concatenate([ref[1] for ref in piece_refs], axis=0)
        heads = dot(incoming, output_ref[...]).astype(BF16)
        for j in range(count):
            out_ref, rows = outs[j % 2], half_rows(me_ref, j, count, seq)
            place = slice(j * seq, (j + 1) * seq)
            out_ref[rows, :wide] = projected[place]
            out_ref[rows, wide:] = heads[place]
        sums = jnp.sum(project.astype(F32), axis=0, keepdims=True) / width
        place = lax.broadcasted_iota(jnp.int32, (extra, LANES), 0) - 2 * ticks * (me_ref[0] // 2)
        facts = jnp.zeros((extra, LANES), F32)
        for t in range(ticks):
            for index, value in enumerate(split_two(as_row(scale_refs[t][...]))):
                facts = jnp.where(place == 2 * t + index, value, facts)
        for out_ref, lanes in zip(outs, (facts, jnp.zeros((extra, LANES), F32))):
            out_ref[half * seq :, :LANES] = lanes.astype(BF16)
            out_ref[half * seq :, LANES:] = two_terms(sums, extra)

    outs = [shape(half * seq + extra, wide + head)] * 2
    return kernel_call(body, outs, [me], [*pieces, *scales, project, output])


def half_rows(me_ref, j, count, seq):
    block = replica_of(me_ref, j, count) // 2
    return pl.ds(pl.multiple_of(block * seq, seq), seq)


def later_partials(pieces, project, me):
    count = len(pieces)
    seq = pieces[0].shape[0]
    wide = project.shape[1]

    def body(me_ref, *refs):
        piece_refs, (project_ref, *outs) = refs[:count], refs[count:]
        hidden = jnp.concatenate([ref[...] for ref in piece_refs], axis=0)
        value = dot(hidden, project_ref[...]).astype(BF16)
        for j in range(count):
            rows = half_rows(me_ref, j, count, seq)
            outs[j % 2][rows, :] = value[j * seq : (j + 1) * seq]

    return kernel_call(body, [shape(count // 2 * seq, wide)] * 2, [me], [*pieces, project])


def two_terms(row, rows):
    high, low = split_two(row)
    place = lax.broadcasted_iota(jnp.int32, (rows, row.shape[1]), 0)
    return jnp.where(place % 2 == 0, high, low).astype(BF16)


def add_two(left, right, tail=None):
    def body(left_ref, right_ref, out_ref):
        total = left_ref[...].astype(F32) + right_ref[...].astype(F32)
        out_ref[...] = total.astype(BF16)
        if tail is not None:
            means = total[tail : tail + 1, LANES:] + total[tail + 1 : tail + 2, LANES:]
            out_ref[tail:, LANES:] = two_terms(means, left.shape[0] - tail)

    return kernel_call(body, [shape(*left.shape)], [], [left, right])[0]


def attention_back(projected, head_half, row_mean, scale, seq, outs, width):
    grad_ref, mixed_ref, numbers_ref = outs
    rows, head = head_half.shape
    count = rows // seq
    root = math.sqrt(head)
    query, query_scale = normalize(projected[:, :head])
    key, key_scale = normalize(projected[:, head : 2 * head])
    query_half, key_half = query.astype(BF16), key.astype(BF16)
    value_half = projected[:, 2 * head :].astype(BF16)

    def each(function, *values):
        return jnp.concatenate(
            [function(*(v[r * seq : (r + 1) * seq] for v in values)) for r in range(count)], axis=0
        )

    def last(left, right):
        return dot(left, right, CONTRACT_LAST)

    def leading(left, right):
        return dot(left, right, CONTRACT_FIRST)

    powered = jnp.exp(each(last, query_half, key_half) / root)
    attention = powered / jnp.sum(powered, axis=-1, keepdims=True)
    attention_half = attention.astype(BF16)
    mixed_ref[...] = each(dot, attention_half, value_half).astype(BF16)
    prob_grad = each(last, head_half, value_half)
    value_grad = each(leading, attention_half, head_half).astype(BF16)
    score_grad = (
        attention * (prob_grad - jnp.sum(attention * prob_grad, axis=-1, keepdims=True)) / root
    ).astype(BF16)
    query_grad = norm_back(each(dot, score_grad, key_half), query, query_scale)
    key_grad = norm_back(each(leading, score_grad, query_half), key, key_scale)
    proj_grad = jnp.concatenate(
        [query_grad.astype(BF16), key_grad.astype(BF16), value_grad], axis=1
    )
    grad_ref[...] = proj_grad
    spread = proj_grad.astype(F32)
    offset = scale * jnp.sum(spread * row_mean, axis=-1, keepdims=True)
    slope = scale * (jnp.sum(spread * projected, axis=-1, keepdims=True) / width)
    lane = lax.broadcasted_iota(jnp.int32, (rows, LANES), 1)
    numbers_ref[...] = jnp.where(lane == 0, scale, jnp.where(lane == 1, offset, slope))
    return proj_grad, slope


def all_rows(half_refs, seq, half, columns):
    return jnp.concatenate([ref[: half * seq, columns] for ref in half_refs], axis=0).astype(F32)


def scale_column(half_refs, tick, ticks, seq, half):
    columns = []
    for ref in half_refs:
        facts = ref[half * seq :, :LANES].astype(F32)
        for block in range(half):
            row = 2 * (ticks * block + tick)
            columns.append(column(facts[row : row + 1] + facts[row + 1 : row + 2])[:seq, :1])
    return jnp.concatenate(columns, axis=0)


def row_means(half_refs, seq, half):
    facts = half_refs[0][half * seq :, LANES:].astype(F32)
    return facts[:1] + facts[1:2]


def attention_outs(rows, head):
    return [shape(rows, 3 * head), shape(rows, head), shape(rows, LANES, kind=F32)]


def below_parts(pieces, project, below, me):
    count, (_, seq, part) = len(pieces), pieces[0].shape
    wide, head = project.shape[1], below.shape[1]

    def body(me_ref, *refs):
        piece_refs, refs = refs[:count], refs[count:]
        project_ref, below_ref, rows_ref, product_ref, sums_ref = refs
        below = below_ref[...]
        for j in range(count):
            rows = block_rows(me_ref, j, count, seq)
            rows_ref[rows, :head] = dot(piece_refs[j][1], below)
            rows_ref[rows, head:] = dot(piece_refs[j][0], below)
        product_ref[...] = dot(project_ref[...], below, CONTRACT_FIRST)
        sums = jnp.sum(below.astype(F32), axis=0, keepdims=True)
        sums_ref[...] = jnp.broadcast_to(sums, sums_ref.shape)

    outs = [
        shape(count * seq, 2 * head, kind=F32),
        shape(wide, head, kind=F32),
        shape(8, head, kind=F32),
    ]
    return kernel_call(body, outs, [me], [*pieces, project, below])


def first_attention(halves, parts, tops, below, seq, half, head, ticks, me, first, width):
    rows, wide, count, runs = 2 * half * seq, 3 * head, 2 * half, len(tops)
    run = below.shape[0] // runs

    def body(me_ref, first_ref, *refs):
        mine, (rows_ref, product_ref, sums_ref), refs = refs[:2], refs[2:5], refs[5:]
        top_refs, (below_ref, *outs, head_ref) = refs[:runs], refs[runs:]
        scale = scale_column(mine, 0, ticks, seq, half)
        row_mean = row_means(mine, seq, half)
        proj_grad, slope = attention_back(
            all_rows(mine, seq, half, slice(0, wide)),
            all_rows(mine, seq, half, slice(wide, wide + head)).astype(BF16),
            row_mean,
            scale,
            seq,
            outs,
            width,
        )
        centered = [
            product_ref[start : start + LANES, :]
            - column(row_mean[:, start : start + LANES])[:, :1] * sums_ref[:1, :]
            for start in range(0, wide, LANES)
        ]
        across = dot(proj_grad, jnp.concatenate(centered, axis=0).astype(BF16))
        change = scale * across - slope * rows_ref[:, head:]
        heads = (rows_ref[:, :head] + change).astype(BF16)
        for parity in range(2):
            for block in range(half):
                replica = 2 * block + lax.rem(me_ref[0] + parity, 2)
                start = (parity * half + block) * seq
                place = pl.ds(pl.multiple_of(replica * seq, seq), seq)
                head_ref[place, :] = heads[start : start + seq]

        @pl.when(first_ref[0] == 1)
        def _():
            for block in range(count):
                replica = lax.bitwise_xor(me_ref[0], block)
                place = pl.ds(pl.multiple_of(replica * seq, seq), seq)
                head_ref[place, :] = sum(
                    dot(top_refs[a][block], below_ref[a * run : (a + 1) * run, :])
                    for a in range(runs)
                ).astype(BF16)

    outs = [*attention_outs(rows, head), shape(rows, head)]
    arrays = [*halves, *parts, *tops, below]
    return kernel_call(body, outs, [me, first], arrays)


def sum_heads(heads, seq, me):
    rows, head = heads[0].shape
    half = rows // seq // 2

    def body(me_ref, *refs):
        for parity in range(2):
            for block in range(half):
                replica = 2 * block + lax.rem(me_ref[0] + parity, 2)
                place = pl.ds(pl.multiple_of(replica * seq, seq), seq)
                total = sum(ref[place, :].astype(F32) for ref in refs[:-1])
                start = (parity * half + block) * seq
                refs[-1][start : start + seq, :] = total.astype(BF16)

    return kernel_call(body, [shape(rows, head)], [me], heads, cost=1)[0]


def later_attention(halves, facts, head_half, seq, half, head, ticks, width):
    rows = 2 * half * seq

    def body(*refs):
        mine, facts, (head_ref, *outs) = refs[:2], refs[2:4], refs[4:]
        attention_back(
            all_rows(mine, seq, half, slice(None)),
            head_ref[...],
            row_means(facts, seq, half),
            scale_column(facts, 1, ticks, seq, half),
            seq,
            outs,
            width,
        )

    arrays = [*halves, *facts, head_half]
    return kernel_call(body, attention_outs(rows, head), [], arrays, cost=1)


def input_gradient(hidden_grad, numbers, incoming, hidden):
    scale, offset, slope = (numbers[:, i : i + 1] for i in range(3))
    change = scale * hidden_grad - offset - slope * hidden.astype(F32)
    return (incoming.astype(F32) + change).astype(BF16)


def middle_step(grads, pieces, tops, project, me, first):
    count, (_, seq, part) = len(pieces), pieces[0].shape
    runs = len(tops)
    run = part // runs

    def body(me_ref, first_ref, *refs):
        top_refs, piece_refs, refs = refs[:runs], refs[runs : runs + count], refs[runs + count :]
        grad_ref, numbers_ref, project_ref, passed_ref, sems, wide_ref = refs
        is_first = first_ref[0] == 1

        @pl.when(is_first)
        def _():
            copies = []
            for j in range(count):
                block = lax.bitwise_xor(me_ref[0], replica_of(me_ref, j, count))
                for a in range(runs):
                    place = passed_ref.at[j, :, pl.ds(a * run, run)]
                    copies.append(
                        pltpu.make_async_copy(top_refs[a].at[block], place, sems.at[j, a])
                    )
                    copies[-1].start()
            for copy in copies:
                copy.wait()

        @pl.when(jnp.logical_not(is_first))
        def _():
            wide_ref[...] = dot(grad_ref[...], project_ref[...], CONTRACT_LAST)
            for j in range(count):
                rows = block_rows(me_ref, j, count, seq)
                hidden, incoming = piece_refs[j][0], piece_refs[j][1]
                passed_ref[j] = input_gradient(
                    wide_ref[rows, :], numbers_ref[rows, :], incoming, hidden
                )

    scratch = [
        pltpu.SemaphoreType.DMA((count, runs)),
        pltpu.VMEM((count * seq, part), F32),
    ]
    arrays = [*pieces, *grads, project]
    outs = [shape(count, seq, part)]
    return kernel_call(body, outs, [me, first], arrays, scratch, far=tops)[0]


def last_step(grads, received, pieces, project, me):
    count, (seq, part) = len(pieces), pieces[0].shape

    def body(me_ref, *refs):
        piece_refs, refs = refs[:count], refs[count:]
        grad_ref, numbers_ref, received_ref, project_ref, *outs, wide_ref = refs
        wide_ref[...] = dot(grad_ref[...], project_ref[...], CONTRACT_LAST)
        for j in range(count):
            rows = block_rows(me_ref, j, count, seq)
            outs[j][...] = input_gradient(
                wide_ref[rows, :], numbers_ref[rows, :], received_ref[j], piece_refs[j][...]
            )

    arrays = [*pieces, *grads, received, project]
    scratch = [pltpu.VMEM((count * seq, part), F32)]
    return list(kernel_call(body, [shape(seq, part)] * count, [me], arrays, scratch))


def weight_gradients(pieces, later, received, first_grads, later_grads, me):
    count, (_, seq, part) = len(pieces), pieces[0].shape
    wide, head = first_grads[0].shape[1], first_grads[1].shape[1]
    block = min(part, 256)

    def body(me_ref, *refs):
        piece_refs, later_refs, refs = refs[:count], refs[count : 2 * count], refs[2 * count :]
        received_ref, grad0, mixed0, grad1, mixed1, project_ref, output_ref = refs
        for start in range(0, part, block):
            columns = slice(start, start + block)
            project_sum, output_sum = 0.0, 0.0
            for j in range(count):
                rows = block_rows(me_ref, j, count, seq)
                value = dot(piece_refs[j][0, :, columns], grad0[rows, :], CONTRACT_FIRST)
                value += dot(later_refs[j][:, columns], grad1[rows, :], CONTRACT_FIRST)
                project_sum += value.astype(BF16).astype(F32)
                value = dot(piece_refs[j][1, :, columns], mixed0[rows, :], CONTRACT_FIRST)
                value += dot(received_ref[j, :, columns], mixed1[rows, :], CONTRACT_FIRST)
                output_sum += value.astype(BF16).astype(F32)
            project_ref[columns, :] = project_sum
            output_ref[columns, :] = output_sum

    outs = [shape(part, wide, kind=F32), shape(part, head, kind=F32)]
    arrays = [*pieces, *later, received, *first_grads, *later_grads]
    return kernel_call(body, outs, [me], arrays)


def join_features(pieces, me):
    count = len(pieces)
    seq, part = pieces[0].shape

    def body(me_ref, *refs):
        for j in range(count):
            owner = lax.rem(me_ref[0] + j, count)
            columns = pl.ds(pl.multiple_of(owner * part, LANES), part)
            refs[count][:, columns] = refs[j][...]

    return kernel_call(body, [shape(seq, part * count)], [me], pieces)[0]


def shift(value, steps):
    count = lax.axis_size("dp")
    if steps % count == 0:
        return value
    return lax.ppermute(value, "dp", [(i, (i + steps) % count) for i in range(count)])


def after(value, *earlier):
    return lax.optimization_barrier((value, *earlier))[0]


def down(value, steps=0):
    pipe, count = lax.axis_size("pipe"), lax.axis_size("dp")
    pairs = [
        (p * count + r, (p - 1) % pipe * count + (r + steps) % count)
        for p in range(pipe)
        for r in range(count)
    ]
    return lax.ppermute(value, BOTH, pairs)


def join_pieces(left, right):
    size = left.shape[0]

    def body(left_ref, right_ref, out_ref):
        out_ref[:size] = left_ref[...]
        out_ref[size:] = right_ref[...]

    outs = [shape(2 * size, *left.shape[1:])]
    return kernel_call(body, outs, [], [left, right])[0]


def toward_owner(blocks, bit):
    pipe, count = lax.axis_size("pipe"), lax.axis_size("dp")
    runs = pipe // count
    pairs = [
        (q * count + r, q * count + (r ^ bit))
        for q in range(pipe)
        for r in range(count)
        if (r ^ (q // runs)) % (2 * bit) == bit
    ]
    return lax.ppermute(blocks, BOTH, pairs)


def owner_to_first(blocks, run):
    pipe, count = lax.axis_size("pipe"), lax.axis_size("dp")
    runs = pipe // count
    return lax.ppermute(blocks, BOTH, [((runs * s + run) * count + s, s) for s in range(count)])


def exchanged(value, step):
    count = lax.axis_size("dp")
    return lax.ppermute(value, "dp", [(i, i ^ step) for i in range(count)])


def shards(section_inputs, arriving, top_grads, project_weights, output_weights):
    count = lax.axis_size("dp")
    pipe = lax.axis_size("pipe")
    me = lax.axis_index("dp")
    first = lax.axis_index("pipe") == 0
    _, ticks, seq, width = section_inputs.shape
    head = output_weights.shape[2]
    project, output = project_weights[0], output_weights[0]
    others, half = range(count), count // 2

    blocks, moved = top_grads, toward_owner(top_grads, 1)
    sent, scale = first_pieces(section_inputs[0], arriving[0], me, count)
    pieces = [shift(sent[j], j) for j in others]
    later_sent, later_scale = later_pieces(section_inputs[0], me, count)
    blocks = join_pieces(after(blocks, scale), moved)
    bit = 2
    while bit < count // 2:
        blocks = join_pieces(blocks, toward_owner(blocks, bit))
        bit *= 2
    moved = toward_owner(blocks, bit) if bit < count else None

    mine, other = first_partials(
        pieces, [scale, later_scale], after(project, blocks), output, me, width
    )
    below = lax.ppermute(
        after(output, other), "pipe", [(p, (p + 1) % pipe) for p in range(pipe)]
    )
    later_sent = after(tuple(later_sent), other)
    later = [shift(later_sent[j], j) for j in others]
    early = [later[j] for j in [2] if j < count]
    total = add_two(after(mine, below, *early), exchanged(other, 1), half * seq)
    if moved is not None:
        blocks = join_pieces(after(blocks, total), moved)
    tops = [owner_to_first(blocks, run) for run in range(pipe // count)]
    later_mine, later_other = later_partials(later, project, me)
    parts = below_parts(pieces, project, below, me)
    step = 2
    while step < count:
        received = exchanged(total, step)
        total = add_two(after(total, later_other), received, half * seq)
        step *= 2
    halves = [total, exchanged(total, 1)]
    later_total = add_two(later_mine, exchanged(later_other, 1))
    halves[0] = after(halves[0], later_total)
    later_parts, step = [later_total], 2
    while step < count:
        later_parts = [later_total, exchanged(later_total, step)]
        later_total = add_two(*later_parts)
        step *= 2

    *first_grads, heads = first_attention(
        halves, parts, tops, below, seq, half, head, ticks, me, first, width
    )
    heads = [down(heads, j) for j in others]
    later_halves = [later_total, exchanged(later_total, 1)]
    passed = middle_step([first_grads[0], first_grads[2]], pieces, tops, project, me, first)
    received = down(after(passed, later_parts[-1]))
    head_half = sum_heads(heads, seq, me)
    later_grads = later_attention(
        later_halves, halves, head_half, seq, half, head, ticks, width
    )
    back = last_step([later_grads[0], later_grads[2]], received, later, project, me)
    mixed = after(later_grads[1], back[0])
    back = [shift(back[j], -j) for j in others]
    project_grads, output_grads = weight_gradients(
        pieces, later, received, first_grads[:2], [later_grads[0], mixed], me
    )
    passed_back = join_features(back, me)
    return (project_grads[None], output_grads[None], passed_back[None])


def solution(mesh):
    in_specs = (
        P("pipe", None, "dp", None),
        P("pipe", "dp", None),
        P(None, "dp", "pipe"),
        P("pipe", "dp", None),
        P("pipe", "dp", None),
    )
    out_specs = (P("pipe", "dp", None), P("pipe", "dp", None), P("pipe", "dp", None))
    return jax.shard_map(shards, mesh=mesh, in_specs=in_specs, out_specs=out_specs, check_vma=False)
```
